256 devices in a mesh: gx: 16 (over z, core), gy: 16 (over y, x).
Axes of the slice: x: 4, y: 4, z: 8, core: 2. Of those that a mesh axis runs over, the one named last changes fastest.
Arguments:
- basis: float32 [16, 16, 96, 2048], P('gx', 'gy')
- block_vals: float32 [16, 16, 16, 5, 128, 128], P('gx', 'gy'), as said below
- block_cols: int32 [16, 16, 16, 5], P('gx', 'gy'), may hold values from 0 to 15, as said below
- edge_rows: int32 [16, 16, 4, 256], P('gx', 'gy'), may hold values from 0 to 2047, as said below
- live_counts: int32 [16, 16], P('gx', 'gy'), may hold values from 1024 to 2048, as said below
Outputs:
- encoding: float32 [16, 16, 96, 2048], P('gx', 'gy')
The draws below stay inside these ranges and needn't reach their ends.
Inputs may be any that keep to these rules, and one draw needn't show every extreme that they name: `live_counts`: every tile has 1024 or more live cells, and some tile is full. `block_cols`: entries name blocks of the same tile. `block_vals`: weights are nonnegative; the weight between two cells is the same in both stored blocks that hold it, and a cell has no weight to itself. `edge_rows`: every entry is a live cell of its tile.
All inputs are finite; a program needn't handle non-finite values.
Results may differ from the reference program's by a relative error of at most 0.0001.
Values sent between devices are 32-bit elements; how exact they have to be, the bound alone decides.
A program may use at most 64 MiB of HBM per device.

```python
import math
import jax
import jax.numpy as jnp
from jax import lax

K = 96
BLK = 128
NB = 16
NNZB = 5
HB = 256
DEGREE = 4
CELLS_DEV = 2048
TOTAL_CELLS = 524288
N_GX = 16
N_GY = 16


def tile_offsets(key):
    key_score = jax.random.fold_in(key, 11)
    choices_count = NB // 2 - 1
    scores = jax.random.randint(key_score, (N_GX, N_GY, choices_count), 0, 1 << 20) * choices_count
    scores = scores + lax.iota(jnp.int32, choices_count)[None, None, :]
    order = jnp.argsort(scores, axis=-1, stable=True).astype(jnp.int32)
    return (order[:, :, 0] + 1, order[:, :, 1] + 1)


def tile_counts(key):
    key_raw, key_full = jax.random.split(jax.random.fold_in(key, 23))
    raw_counts = jax.random.randint(key_raw, (N_GX * N_GY,), CELLS_DEV // 2, CELLS_DEV + 1)
    full_tile = jax.random.randint(key_full, (), 0, N_GX * N_GY)
    raw_counts = jnp.where(jnp.arange(N_GX * N_GY, dtype=jnp.int32) == full_tile, CELLS_DEV, raw_counts)
    return raw_counts.reshape(N_GX, N_GY).astype(jnp.int32)


def shifted_blocks(stack_blocks, offsets):
    source = (lax.iota(jnp.int32, NB)[None, :] - offsets.reshape(-1)[:, None]) % NB
    return jnp.take_along_axis(stack_blocks, source[:, :, None, None], axis=1)


def draw_live_counts(key, part):
    return tile_counts(key)


def draw_block_cols(key, part):
    first, second = tile_offsets(key)
    zeros_shift = jnp.zeros_like(first)
    shifts = jnp.stack([zeros_shift, first, -first, second, -second], -1)[:, :, None, :]
    base_rows = lax.iota(jnp.int32, NB)[None, None, :, None]
    return ((base_rows + shifts) % NB).astype(jnp.int32)


def draw_edge_rows(key, part):
    counts = tile_counts(key)
    key_rows, key_place = jax.random.split(jax.random.fold_in(key, 53))
    raw_rows = jax.random.randint(key_rows, (N_GX, N_GY, 4 * HB), 0, counts[:, :, None])
    place = jax.random.randint(key_place, (N_GX, N_GY, 1), 0, 4 * HB)
    raw_rows = jnp.where(lax.iota(jnp.int32, 4 * HB)[None, None, :] == place, counts[:, :, None] - 1, raw_rows)
    return raw_rows.reshape(N_GX, N_GY, 4, HB).astype(jnp.int32)


def draw_block_vals(key, part):
    first, second = tile_offsets(key)
    key_size, key_keep = jax.random.split(jax.random.fold_in(key, 37))
    shape = (N_GX * N_GY, NB, 3, BLK, BLK)
    magnitude = jax.random.uniform(key_size, shape, jnp.float32, 0.5, 1.5)
    growth = 3.0
    raw_weights = magnitude * jax.random.bernoulli(key_keep, 0.25, shape).astype(jnp.float32)
    own_block = raw_weights[:, :, 0]
    own_block = 0.5 * (own_block + jnp.swapaxes(own_block, -1, -2)) * (1.0 - jnp.eye(BLK, dtype=jnp.float32))
    forward_first = raw_weights[:, :, 1]
    forward_second = raw_weights[:, :, 2]
    back_first = jnp.swapaxes(shifted_blocks(forward_first, first), -1, -2)
    back_second = jnp.swapaxes(shifted_blocks(forward_second, second), -1, -2)
    stacked = jnp.stack([own_block, forward_first, back_first, forward_second, back_second], axis=2)
    row_place = lax.iota(jnp.float32, N_GX) / max(N_GX - 1, 1)
    col_place = lax.iota(jnp.float32, N_GY) / max(N_GY - 1, 1)
    density = (growth ** (0.5 * (row_place[:, None] + col_place[None, :]))).reshape(-1) / 40.0
    stacked = stacked * density[:, None, None, None, None]
    return stacked.reshape(N_GX, N_GY, NB, NNZB, BLK, BLK)


def draw_basis(key, part):
    key_base, key_cols, key_rows = jax.random.split(jax.random.fold_in(key, 41), 3)
    shape = (N_GX, N_GY, K, CELLS_DEV)
    column_scale = jnp.exp(jax.random.uniform(key_cols, (K,), jnp.float32, 0.0, math.log(10.0)))
    row_scale = jnp.exp(jax.random.uniform(key_rows, (N_GX, N_GY, 1, CELLS_DEV), jnp.float32, 0.0, math.log(10.0)))
    base_values = jax.random.normal(key_base, shape, jnp.float32)
    return base_values * column_scale[None, None, :, None] * row_scale


def setup_inputs(seed: int = 0) -> dict:
    key_list = jax.random.split(jax.random.key(seed), 6)
    basis = draw_basis(jax.random.fold_in(key_list[5], 71), 0)
    block_vals = draw_block_vals(jax.random.fold_in(key_list[5], 71), 0)
    block_cols = draw_block_cols(jax.random.fold_in(key_list[5], 71), 0)
    edge_rows = draw_edge_rows(jax.random.fold_in(key_list[5], 71), 0)
    live_counts = draw_live_counts(jax.random.fold_in(key_list[5], 71), 0)
    return {"basis": basis, "block_vals": block_vals, "block_cols": block_cols, "edge_rows": edge_rows, "live_counts": live_counts}


PRECISE = lax.Precision.HIGHEST
LOWER_FRACTION = 0.125

def block_product(tile_weights, tile_columns, values):
    vec_count = values.shape[0]
    block_view = values.reshape(vec_count, NB, BLK)
    picked_blocks = jnp.take(block_view, tile_columns.reshape(-1), axis=1).reshape(vec_count, NB, NNZB, BLK)
    product = jnp.einsum('knjc,njrc->knr', picked_blocks, tile_weights, precision=PRECISE)
    return product.reshape(vec_count, NB * BLK)

def reference(basis, block_vals, block_cols, edge_rows, live_counts):
    tile_count = N_GX * N_GY
    weights = block_vals.reshape(tile_count, NB, NNZB, BLK, BLK)
    columns = block_cols.reshape(tile_count, NB, NNZB)
    edge_lists = edge_rows.reshape(tile_count, 4 * HB)
    live_mask = (lax.iota(jnp.int32, CELLS_DEV)[None, :] < live_counts.reshape(tile_count, 1)).astype(jnp.float32)
    tile_row = jnp.arange(N_GX, dtype=jnp.int32)[:, None] * jnp.ones((1, N_GY), jnp.int32)
    tile_col = jnp.ones((N_GX, 1), jnp.int32) * jnp.arange(N_GY, dtype=jnp.int32)[None, :]
    has_neighbour = jnp.stack([tile_row > 0, tile_row < N_GX - 1, tile_col > 0, tile_col < N_GY - 1], -1)
    has_neighbour = has_neighbour.astype(jnp.float32).reshape(tile_count, 4)

    def count_edges(tile_lists, tile_flags):
        return jnp.zeros((CELLS_DEV,), jnp.float32).at[tile_lists].add(jnp.repeat(tile_flags, HB))
    cross_count = jax.vmap(count_edges)(edge_lists, has_neighbour)

    def mask_sum(packed):
        return block_product(packed[0], packed[1], packed[2][None])[0]
    own_sum = lax.map(mask_sum, (weights, columns, live_mask))
    degree = live_mask * (own_sum + cross_count)
    upper_bound = 2.0 * jnp.max(degree)

    def take_edges(values, tile_lists):
        return jnp.take(values, tile_lists, axis=1)

    def add_edges(tile_lists, incoming):
        return jnp.zeros((K, CELLS_DEV), jnp.float32).at[:, tile_lists].add(incoming)

    def crossing(values):
        outgoing = jax.vmap(take_edges)(values, edge_lists).reshape(N_GX, N_GY, K, 4, HB)
        zero_row = jnp.zeros_like(outgoing[:1, :, :, 0])
        zero_col = jnp.zeros_like(outgoing[:, :1, :, 0])
        from_low_x = jnp.concatenate([zero_row, outgoing[:-1, :, :, 1]], 0)
        from_high_x = jnp.concatenate([outgoing[1:, :, :, 0], zero_row], 0)
        from_low_y = jnp.concatenate([zero_col, outgoing[:, :-1, :, 3]], 1)
        from_high_y = jnp.concatenate([outgoing[:, 1:, :, 2], zero_col], 1)
        incoming = jnp.stack([from_low_x, from_high_x, from_low_y, from_high_y], 3).reshape(tile_count, K, 4 * HB)
        return jax.vmap(add_edges)(edge_lists, incoming)

    def local_part(packed):
        return block_product(packed[0], packed[1], packed[2])

    def operator(values):
        inside = lax.map(local_part, (weights, columns, values))
        return live_mask[:, None, :] * (degree[:, None, :] * values - inside - crossing(values))
    lower_edge = LOWER_FRACTION * upper_bound
    half_width = (upper_bound - lower_edge) / 2.0
    centre = (upper_bound + lower_edge) / 2.0
    previous = live_mask[:, None, :] * basis.reshape(tile_count, K, CELLS_DEV)
    current = (operator(previous) - centre * previous) / half_width
    for repeat in range(DEGREE - 1):
        following = 2.0 / half_width * (operator(current) - centre * current) - previous
        previous = current
        current = following
    gram = jnp.einsum('tkc,tlc->kl', current, current, precision=PRECISE)
    factor_lower = jnp.linalg.cholesky(gram)
    inverse = jax.scipy.linalg.solve_triangular(factor_lower, jnp.eye(K, dtype=jnp.float32), lower=True)
    encoding = jnp.einsum('kl,tlc->tkc', inverse, current, precision=PRECISE) * math.sqrt(TOTAL_CELLS)
    return encoding.reshape(N_GX, N_GY, K, CELLS_DEV)
```

```python
import math

import jax
import jax.numpy as jnp
from jax import lax
from jax.experimental import pallas as pl
from jax.experimental.pallas import tpu as pltpu
from jax.sharding import PartitionSpec as P

LOWER_FRACTION = 0.125
MESH = pl.DeviceIdType.MESH
F32 = jnp.float32
BF16 = jnp.bfloat16
NN = (((1,), (0,)), ((), ()))
NT = (((1,), (1,)), ((), ()))


def dot(a, b, dims=NN):
    return lax.dot_general(a, b, dims, preferred_element_type=F32)


def split(x):
    hi = x.astype(BF16)
    lo = (x - hi.astype(F32)).astype(BF16)
    return hi, lo


def inverse_factor(gram_ref, elem_ref, out_ref, scale, rows):
    blocks = rows // 8
    lane = lax.broadcasted_iota(jnp.int32, (8, 128), 1)

    def across(col):
        return jnp.broadcast_to(col, (8, 128))

    for b in range(blocks):
        first = 8 * b
        cols = {}
        for i in range(b, blocks):
            tile = gram_ref[i]
            cols[i] = [across(tile[:, first + k : first + k + 1]) for k in range(8)]
        for k in range(8):
            elem_ref[k] = cols[b][k]
        a = {
            (i, k): across(elem_ref[k, i : i + 1, :]) for k in range(8) for i in range(k, 8)
        }
        inside = (lane >= first) & (lane < first + 8)
        reduced = []
        for k in range(8):
            row = across(gram_ref[b, k : k + 1, :])
            reduced.append(jnp.where(inside, jnp.where(lane == first + k, 1.0, 0.0), row))
        inv = []
        low = {}
        for k in range(8):
            inv.append(1.0 / a[k, k])
            for i in range(k + 1, 8):
                low[i, k] = a[i, k] * inv[k]
                for j in range(k + 1, i + 1):
                    a[i, j] = a[i, j] - low[i, k] * a[j, k]
                reduced[i] = reduced[i] - low[i, k] * reduced[k]
        for i in range(b + 1, blocks):
            u = cols[i]
            for k in range(8):
                for j in range(k + 1, 8):
                    u[j] = u[j] - low[j, k] * u[k]
            tile = jnp.where(inside, 0.0, gram_ref[i])
            for k in range(8):
                tile = tile - (u[k] * inv[k]) * reduced[k]
            gram_ref[i] = tile
        for k in range(8):
            row = jnp.where(lane <= first + k, reduced[k], 0.0) * (lax.rsqrt(a[k, k]) * scale)
            out_ref[first + k : first + k + 1, :] = row[0:1, :]


def kernel(
    size_x,
    size_y,
    live_ref,
    cols_ref,
    basis_ref,
    edges_ref,
    vals_ref,
    out_ref,
    raw,
    wts,
    pick,
    place,
    vp,
    vm,
    inp,
    y0,
    ay0,
    z,
    y2,
    acc,
    deg,
    mask,
    sbuf,
    rbuf,
    mxa,
    mxb,
    gpart,
    gr1,
    gr2,
    gfull,
    elem,
    inv,
    wsem,
    hs,
    hr,
    cs,
    cr,
):
    me_x = lax.axis_index("gx")
    me_y = lax.axis_index("gy")
    blocks, stored = cols_ref.shape[2], cols_ref.shape[3]
    block = vals_ref.shape[-1]
    vecs, cells = basis_ref.shape[2], basis_ref.shape[3]
    sides, edges = edges_ref.shape[2], edges_ref.shape[3]
    group_rows = 2 * vecs

    def peer_x(d):
        return {"gx": lax.rem(me_x + d, size_x), "gy": me_y}

    def peer_y(d):
        return {"gx": me_x, "gy": lax.rem(me_y + d, size_y)}

    barrier = pltpu.get_barrier_semaphore()
    for d in range(1, size_x):
        pl.semaphore_signal(barrier, inc=1, device_id=peer_x(d), device_id_type=MESH)
    for d in range(1, size_y):
        pl.semaphore_signal(barrier, inc=1, device_id=peer_y(d), device_id_type=MESH)

    fetches = [
        pltpu.make_async_copy(vals_ref.at[0, 0, n], raw.at[n], wsem.at[n]) for n in range(blocks)
    ]
    for f in fetches:
        f.start()

    has = [me_x > 0, me_x < size_x - 1, me_y > 0, me_y < size_y - 1]
    target = [
        {"gx": me_x - 1, "gy": me_y},
        {"gx": me_x + 1, "gy": me_y},
        {"gx": me_x, "gy": me_y - 1},
        {"gx": me_x, "gy": me_y + 1},
    ]
    facing = [1, 0, 3, 2]

    def halo(app, side):
        return pltpu.make_async_remote_copy(
            src_ref=sbuf.at[app, side],
            dst_ref=rbuf.at[app, facing[side]],
            send_sem=hs.at[app, side],
            recv_sem=hr.at[app, facing[side]],
            device_id=target[side],
            device_id_type=MESH,
        )

    for side in range(sides):

        @pl.when(jnp.logical_not(has[side]))
        def _(side=side):
            for app in range(4):
                rbuf[app, side] = jnp.zeros((vecs, edges), F32)

    lane_id = lax.broadcasted_iota(jnp.int32, (8, cells), 1)
    mask[...] = jnp.where(lane_id < live_ref[0, 0], 1.0, 0.0)
    live = mask[0:1, :]
    start = basis_ref[0, 0] * live
    y0[...] = start

    def store_parts(begin, x):
        hi, lo = split(x)
        for t in range(x.shape[1] // block):
            lanes = slice(t * block, (t + 1) * block)
            vp[begin // block + t, 0:vecs, :] = hi[:, lanes]
            vp[begin // block + t, vecs:group_rows, :] = lo[:, lanes]

    def parts_at(begin, width):
        return jnp.concatenate(
            [vp[t] for t in range(begin // block, (begin + width) // block)], axis=1
        )

    store_parts(0, start)
    wide_live = jnp.broadcast_to(live, (16, cells)).astype(BF16)
    for t in range(blocks):
        vm[t] = wide_live[:, t * block : (t + 1) * block]

    step = 128

    @pl.loop(0, cells // step)
    def _(t):
        base = pl.multiple_of(t * step, step)
        cell = lax.broadcasted_iota(jnp.int32, (step, edges), 0) + base
        for side in range(sides):
            ends = edges_ref[0, 0, side : side + 1, :]
            pick[pl.ds(base, step), side * edges : (side + 1) * edges] = jnp.where(
                cell == ends, 1.0, 0.0
            ).astype(BF16)

    def send(app, pair):
        lanes = slice(pair * 2 * edges, (pair + 1) * 2 * edges)
        got = dot(parts_at(0, cells), pick[:, lanes])
        got = got[0:vecs] + got[vecs:]
        for k in range(2):
            sbuf[app, 2 * pair + k] = got[:, k * edges : (k + 1) * edges]
        for k in range(2):

            @pl.when(has[2 * pair + k])
            def _(k=k):
                halo(app, 2 * pair + k).start()

    def multiply(app, extra):
        for n in range(blocks):
            parts = []
            for s in range(stored):
                at = cols_ref[0, 0, n, s]
                part = vp[at]
                parts.append(jnp.concatenate([part, vm[at]], axis=0) if extra else part)
            got = dot(jnp.concatenate(parts, axis=1), wts[n], NT)
            here = slice(n * block, (n + 1) * block)
            acc[:, here] = got[0:vecs, 0:block] + got[vecs:group_rows, 0:block] + got[0:vecs, block:]
            if extra:
                own = got[group_rows : group_rows + 8, 0:block] + got[group_rows : group_rows + 8, block:]
                deg[:, here] = own

    def receive(app):
        for side in range(sides):

            @pl.when(has[side])
            def _(side=side):
                pltpu.make_async_remote_copy(
                    src_ref=sbuf.at[app, side],
                    dst_ref=rbuf.at[app, side],
                    send_sem=hs.at[app, side],
                    recv_sem=hr.at[app, side],
                    device_id=target[side],
                    device_id_type=MESH,
                ).wait_recv()

        for side in range(sides):
            hi, lo = split(rbuf[app, side])
            lanes = slice(side * edges, (side + 1) * edges)
            inp[0:vecs, lanes] = hi
            inp[vecs:group_rows, lanes] = lo

    chunk = 512
    chunks = [slice(q * chunk, (q + 1) * chunk) for q in range(cells // chunk)]

    def landed(sl, rows):
        return dot(inp[0:rows, :], place[:, sl])

    def exchange(kind, buf, peer, me, size):
        def one(d):
            return pltpu.make_async_remote_copy(
                src_ref=buf.at[me],
                dst_ref=buf.at[me],
                send_sem=cs.at[kind, d],
                recv_sem=cr.at[kind, d],
                device_id=peer(d),
                device_id_type=MESH,
            )

        return [one(d) for d in range(1, size)]

    def wait_from(kind, buf, me, size, peer, d):
        src = lax.rem(me + size - d, size)
        return pltpu.make_async_remote_copy(
            src_ref=buf.at[src],
            dst_ref=buf.at[src],
            send_sem=cs.at[kind, d],
            recv_sem=cr.at[kind, d],
            device_id=peer(d),
            device_id_type=MESH,
        )

    pl.semaphore_wait(barrier, size_x + size_y - 2)
    send(0, 1)
    send(0, 0)

    lane = lax.broadcasted_iota(jnp.int32, (128, 128), 1)
    for at in range(0, sides * edges, 128):
        side, from_edge = at // edges, at % edges
        ends = edges_ref[0, 0, side : side + 1, from_edge : from_edge + 128]
        col = jnp.transpose(jnp.broadcast_to(ends.astype(F32), (8, 128)))[:, 0:1]
        wide = jnp.broadcast_to(col, (128, 128)).astype(jnp.int32)
        for t in range(0, cells, 128):
            place[at : at + 128, t : t + 128] = jnp.where(wide == lane + t, 1.0, 0.0).astype(BF16)

    for side in range(sides):
        flag = jnp.where(has[side], 1.0, 0.0).astype(F32)
        inp[group_rows : group_rows + 16, side * edges : (side + 1) * edges] = jnp.full(
            (16, edges), flag, F32
        ).astype(BF16)

    for n in range(blocks):
        fetches[n].wait()
        for s in range(stored):
            hi, lo = split(raw[n, s])
            wts[n, 0:block, s * block : (s + 1) * block] = hi
            wts[n, block : 2 * block, s * block : (s + 1) * block] = lo

    multiply(0, 16)
    receive(0)
    for sl in chunks:
        got = landed(sl, group_rows + 16)
        av = acc[:, sl] + got[0:vecs] + got[vecs:group_rows]
        d = mask[:, sl] * (deg[:, sl] + got[group_rows : group_rows + 8])
        deg[:, sl] = d
        ay0[:, sl] = av
        first = mask[0:1, sl] * (d[0:1] * y0[:, sl] - av)
        z[:, sl] = first
        store_parts(sl.start, first)
    top = jnp.max(deg[...], axis=1, keepdims=True)
    mxa[me_y] = jnp.broadcast_to(top, (8, 128))
    for c in exchange(0, mxa, peer_y, me_y, size_y):
        c.start()

    send(1, 1)
    send(1, 0)
    for d in range(1, size_y):
        wait_from(0, mxa, me_y, size_y, peer_y, d).wait_recv()
    mxb[me_x] = jnp.max(mxa[...], axis=0)
    for c in exchange(1, mxb, peer_x, me_x, size_x):
        c.start()
    multiply(1, 0)
    receive(1)
    for d in range(1, size_x):
        wait_from(1, mxb, me_x, size_x, peer_x, d).wait_recv()
    upper = 2.0 * jnp.max(mxb[...], axis=0)[0:1, :]
    lower = LOWER_FRACTION * upper
    half_width = (upper - lower) / 2.0
    centre = (upper + lower) / 2.0
    over = 1.0 / half_width
    centre = centre[0:1, 0:1]
    over = over[0:1, 0:1]
    twice = 2.0 * over
    for sl in chunks:
        got = landed(sl, group_rows)
        az = acc[:, sl] + got[0:vecs] + got[vecs:]
        y1 = (z[:, sl] - centre * y0[:, sl]) * over
        ay1 = (az - centre * ay0[:, sl]) * over
        ly1 = mask[0:1, sl] * (deg[0:1, sl] * y1 - ay1)
        second = twice * (ly1 - centre * y1) - y0[:, sl]
        z[:, sl] = y1
        y2[:, sl] = second
        store_parts(sl.start, second)

    previous, current, following = z, y2, y0
    for app in (2, 3):
        send(app, 1)
        send(app, 0)
        multiply(app, 0)
        receive(app)
        for sl in chunks:
            got = landed(sl, group_rows)
            av = acc[:, sl] + got[0:vecs] + got[vecs:]
            lap = mask[0:1, sl] * (deg[0:1, sl] * current[:, sl] - av)
            new = twice * (lap - centre * current[:, sl]) - previous[:, sl]
            following[:, sl] = new
            store_parts(sl.start, new)
        previous, current, following = current, following, previous

    both = parts_at(0, cells)
    full = dot(both, both, NT)
    gram = full[0:vecs, 0:vecs] + full[0:vecs, vecs:] + full[vecs:, 0:vecs] + full[vecs:, vecs:]
    gram = jnp.concatenate([gram, jnp.zeros((vecs, 128 - vecs), F32)], axis=1)
    owners = vecs // 8
    for p in range(owners):
        gpart[p] = gram[8 * p : 8 * p + 8, :]

    def to_owner(p):
        return pltpu.make_async_remote_copy(
            src_ref=gpart.at[p],
            dst_ref=gr1.at[me_y],
            send_sem=cs.at[2, p],
            recv_sem=cr.at[2, me_y],
            device_id={"gx": me_x, "gy": p},
            device_id_type=MESH,
        )

    def from_member(q):
        return pltpu.make_async_remote_copy(
            src_ref=gr1.at[q],
            dst_ref=gr1.at[q],
            send_sem=cs.at[2, q],
            recv_sem=cr.at[2, q],
            device_id={"gx": me_x, "gy": q},
            device_id_type=MESH,
        )

    for p in range(owners):

        @pl.when(me_y != p)
        def _(p=p):
            to_owner(p).start()

    @pl.when(me_y < owners)
    def _():
        gr1[me_y] = gpart[me_y]
        for q in range(size_y):

            @pl.when(me_y != q)
            def _(q=q):
                from_member(q).wait_recv()

        gr2[me_x] = jnp.sum(gr1[...], axis=0)
        for c in exchange(3, gr2, peer_x, me_x, size_x):
            c.start()
        for d in range(1, size_x):
            wait_from(3, gr2, me_x, size_x, peer_x, d).wait_recv()
        gfull[me_y] = jnp.sum(gr2[...], axis=0)
        for c in exchange(4, gfull, peer_y, me_y, size_y):
            c.start()

    def from_owner(p):
        return pltpu.make_async_remote_copy(
            src_ref=gfull.at[p],
            dst_ref=gfull.at[p],
            send_sem=cs.at[4, 0],
            recv_sem=cr.at[4, lax.rem(me_y + size_y - p, size_y)],
            device_id={"gx": me_x, "gy": p},
            device_id_type=MESH,
        )

    for p in range(owners):

        @pl.when(me_y != p)
        def _(p=p):
            from_owner(p).wait_recv()

    for app in range(4):
        for side in range(sides):

            @pl.when(has[side])
            def _(app=app, side=side):
                halo(app, side).wait_send()

    for c in exchange(0, mxa, peer_y, me_y, size_y) + exchange(1, mxb, peer_x, me_x, size_x):
        c.wait_send()
    for p in range(owners):

        @pl.when(me_y != p)
        def _(p=p):
            to_owner(p).wait_send()

    @pl.when(me_y < owners)
    def _():
        for c in exchange(3, gr2, peer_x, me_x, size_x) + exchange(4, gfull, peer_y, me_y, size_y):
            c.wait_send()

    total = cells * size_x * size_y
    inverse_factor(gfull, elem, inv, math.sqrt(total), vecs)
    hi, lo = split(inv[...])
    hi, lo = hi[:, 0:vecs], lo[:, 0:vecs]
    left = jnp.concatenate(
        [jnp.concatenate([hi, hi], axis=1), jnp.concatenate([lo, lo], axis=1)], axis=0
    )
    for sl in chunks:
        got = dot(left, parts_at(sl.start, chunk))
        out_ref[0, 0, :, sl] = got[0:vecs] + got[vecs:]


def per_device(size_x, size_y, basis, block_vals, block_cols, edge_rows, live_counts):
    blocks, stored, block = block_vals.shape[2:5]
    vecs, cells = basis.shape[2:]
    sides, edges = edge_rows.shape[2:]
    vmem = pltpu.VMEM
    field = vmem((vecs, cells), F32)
    scratch = [
        vmem((blocks, stored, block, block), F32),
        vmem((blocks, 2 * block, stored * block), BF16),
        vmem((cells, sides * edges), BF16),
        vmem((sides * edges, cells), BF16),
        vmem((blocks, 2 * vecs, block), BF16),
        vmem((blocks, 16, block), BF16),
        vmem((2 * vecs + 16, sides * edges), BF16),
        field,
        field,
        field,
        field,
        field,
        vmem((8, cells), F32),
        vmem((8, cells), F32),
        vmem((4, sides, vecs, edges), F32),
        vmem((4, sides, vecs, edges), F32),
        vmem((size_y, 8, 128), F32),
        vmem((size_x, 8, 128), F32),
        vmem((vecs // 8, 8, 128), F32),
        vmem((size_y, 8, 128), F32),
        vmem((size_x, 8, 128), F32),
        vmem((vecs // 8, 8, 128), F32),
        vmem((8, 8, 128), F32),
        vmem((vecs, 128), F32),
        pltpu.SemaphoreType.DMA((blocks,)),
        pltpu.SemaphoreType.DMA((4, sides)),
        pltpu.SemaphoreType.DMA((4, sides)),
        pltpu.SemaphoreType.DMA((5, max(size_x, size_y))),
        pltpu.SemaphoreType.DMA((5, max(size_x, size_y))),
    ]
    in_vmem = pl.BlockSpec(memory_space=vmem)
    in_smem = pl.BlockSpec(memory_space=pltpu.SMEM)
    return pl.pallas_call(
        lambda *refs: kernel(size_x, size_y, *refs),
        out_shape=jax.ShapeDtypeStruct(basis.shape, F32),
        in_specs=[in_smem, in_smem, in_vmem, in_vmem, pl.BlockSpec(memory_space=pl.ANY)],
        out_specs=in_vmem,
        scratch_shapes=scratch,
        compiler_params=pltpu.CompilerParams(
            collective_id=0, has_side_effects=True, vmem_limit_bytes=56 * 2**20
        ),
        name="filtered_subspace_step",
    )(live_counts, block_cols, basis, edge_rows, block_vals)


def solution(mesh):
    size_x, size_y = mesh.shape["gx"], mesh.shape["gy"]
    in_specs = (
        P("gx", "gy", None, None),
        P("gx", "gy", None, None, None, None),
        P("gx", "gy", None, None),
        P("gx", "gy", None, None),
        P("gx", "gy"),
    )
    out_specs = P("gx", "gy", None, None)
    return jax.shard_map(
        lambda *args: per_device(size_x, size_y, *args),
        mesh=mesh,
        in_specs=in_specs,
        out_specs=out_specs,
        check_vma=False,
    )
```

```python
import math

import jax
import jax.numpy as jnp
from jax import lax
from jax.experimental import pallas as pl
from jax.experimental.pallas import tpu as pltpu
from jax.sharding import PartitionSpec as P

LOWER_FRACTION = 0.125
MESH = pl.DeviceIdType.MESH
F32 = jnp.float32
BF16 = jnp.bfloat16
NN = (((1,), (0,)), ((), ()))
NT = (((1,), (1,)), ((), ()))


def dot(a, b, dims=NN):
    return lax.dot_general(a, b, dims, preferred_element_type=F32)


def split(x):
    hi = x.astype(BF16)
    lo = (x - hi.astype(F32)).astype(BF16)
    return hi, lo


def inverse_factor(gram_ref, elem_ref, out_ref, scale, rows):
    blocks = rows // 8
    lane = lax.broadcasted_iota(jnp.int32, (8, 128), 1)

    def across(col):
        return jnp.broadcast_to(col, (8, 128))

    for b in range(blocks):
        first = 8 * b
        cols = {}
        for i in range(b, blocks):
            tile = gram_ref[i]
            cols[i] = [across(tile[:, first + k : first + k + 1]) for k in range(8)]
        for k in range(8):
            elem_ref[k] = cols[b][k]
        a = {
            (i, k): across(elem_ref[k, i : i + 1, :]) for k in range(8) for i in range(k, 8)
        }
        inside = (lane >= first) & (lane < first + 8)
        reduced = []
        for k in range(8):
            row = across(gram_ref[b, k : k + 1, :])
            reduced.append(jnp.where(inside, jnp.where(lane == first + k, 1.0, 0.0), row))
        inv = []
        low = {}
        for k in range(8):
            inv.append(1.0 / a[k, k])
            for i in range(k + 1, 8):
                low[i, k] = a[i, k] * inv[k]
                for j in range(k + 1, i + 1):
                    a[i, j] = a[i, j] - low[i, k] * a[j, k]
                reduced[i] = reduced[i] - low[i, k] * reduced[k]
        for i in range(b + 1, blocks):
            u = cols[i]
            for k in range(8):
                for j in range(k + 1, 8):
                    u[j] = u[j] - low[j, k] * u[k]
            tile = jnp.where(inside, 0.0, gram_ref[i])
            for k in range(8):
                tile = tile - (u[k] * inv[k]) * reduced[k]
            gram_ref[i] = tile
        for k in range(8):
            row = jnp.where(lane <= first + k, reduced[k], 0.0) * (lax.rsqrt(a[k, k]) * scale)
            out_ref[first + k : first + k + 1, :] = row[0:1, :]


def filter_kernel(
    size_x,
    size_y,
    live_ref,
    cols_ref,
    basis_ref,
    edges_ref,
    vals_ref,
    vp,
    gfull,
    raw,
    wts,
    pick,
    place,
    same,
    vm,
    inp,
    fa,
    fb,
    rest,
    deg,
    mask,
    sbuf,
    rbuf,
    mxa,
    mxb,
    gpart,
    gr1,
    gr2,
    wsem,
    hs,
    hr,
    cs,
    cr,
):
    me_x = lax.axis_index("gx")
    me_y = lax.axis_index("gy")
    stored, blocks = cols_ref.shape[1], cols_ref.shape[3]
    block = vals_ref.shape[-1]
    vecs, cells = basis_ref.shape[2], basis_ref.shape[3]
    sides, edges = edges_ref.shape[2], edges_ref.shape[3]
    ends_all = sides * edges
    group_rows = 2 * vecs

    def peer_x(d):
        return {"gx": lax.rem(me_x + d, size_x), "gy": me_y}

    def peer_y(d):
        return {"gx": me_x, "gy": lax.rem(me_y + d, size_y)}

    barrier = pltpu.get_barrier_semaphore()
    for d in range(1, size_x):
        pl.semaphore_signal(barrier, inc=1, device_id=peer_x(d), device_id_type=MESH)
    for d in range(1, size_y):
        pl.semaphore_signal(barrier, inc=1, device_id=peer_y(d), device_id_type=MESH)

    fetches = [
        pltpu.make_async_copy(vals_ref.at[0, 0, n], raw.at[n], wsem.at[n]) for n in range(blocks)
    ]
    for f in fetches:
        f.start()

    has = [me_x > 0, me_x < size_x - 1, me_y > 0, me_y < size_y - 1]
    target = [
        {"gx": me_x - 1, "gy": me_y},
        {"gx": me_x + 1, "gy": me_y},
        {"gx": me_x, "gy": me_y - 1},
        {"gx": me_x, "gy": me_y + 1},
    ]
    facing = [1, 0, 3, 2]
    scaled = 1

    def halo(app, side, into):
        rows = vecs + 8 if app == scaled else vecs
        return pltpu.make_async_remote_copy(
            src_ref=sbuf.at[app, side, pl.ds(0, rows)],
            dst_ref=rbuf.at[app, into, pl.ds(0, rows)],
            send_sem=hs.at[app, side],
            recv_sem=hr.at[app, into],
            device_id=target[side],
            device_id_type=MESH,
        )

    for side in range(sides):

        @pl.when(jnp.logical_not(has[side]))
        def _(side=side):
            for app in range(4):
                rbuf[app, side] = jnp.zeros((vecs + 8, edges), F32)

    lane_id = lax.broadcasted_iota(jnp.int32, (8, cells), 1)
    mask[...] = jnp.where(lane_id < live_ref[0, 0], 1.0, 0.0)

    def store_parts(begin, x):
        hi, lo = split(x)
        for t in range(x.shape[1] // block):
            lanes = slice(t * block, (t + 1) * block)
            vp[begin // block + t, 0:vecs, :] = hi[:, lanes]
            vp[begin // block + t, vecs:group_rows, :] = lo[:, lanes]

    def parts_at(begin, width):
        return jnp.concatenate(
            [vp[t] for t in range(begin // block, (begin + width) // block)], axis=1
        )

    start = basis_ref[0, 0] * mask[0:1, :]
    fa[...] = start
    store_parts(0, start)

    step = 128

    @pl.loop(0, cells // step)
    def _(t):
        base = pl.multiple_of(t * step, step)
        cell = lax.broadcasted_iota(jnp.int32, (step, edges), 0) + base
        for side in range(sides):
            ends = edges_ref[0, 0, side : side + 1, :]
            pick[pl.ds(base, step), side * edges : (side + 1) * edges] = jnp.where(
                cell == ends, 1.0, 0.0
            ).astype(BF16)

    chunk = 512
    chunks = [slice(q * chunk, (q + 1) * chunk) for q in range(cells // chunk)]
    pair = 2 * edges

    def gather(k):
        got = dot(parts_at(0, cells), pick[:, k * pair : (k + 1) * pair])
        return got[0:vecs] + got[vecs:]

    def send(app, k, values):
        for i in range(2):
            sbuf[app, 2 * k + i, 0:vecs, :] = values[:, i * edges : (i + 1) * edges]
        for i in range(2):

            @pl.when(has[2 * k + i])
            def _(i=i):
                halo(app, 2 * k + i, facing[2 * k + i]).start()

    def sent(app, k):
        return jnp.concatenate([sbuf[app, 2 * k, 0:vecs, :], sbuf[app, 2 * k + 1, 0:vecs, :]], axis=1)

    def multiply(use, width):
        for n in range(blocks):
            got = dot(
                jnp.concatenate([vp[cols_ref[0, s, 0, n]] for s in range(stored)], axis=1),
                wts[n],
                NT,
            )
            use(
                slice(n * block, (n + 1) * block),
                got[0:vecs, 0:width] + got[vecs:, 0:width] + got[0:vecs, width:],
            )

    def receive(app, factor):
        for side in range(sides):

            @pl.when(has[side])
            def _(side=side):
                halo(app, side, side).wait_recv()

        for side in range(sides):
            came = rbuf[app, side, 0:vecs, :]
            if factor is not None:
                came = came * (rbuf[app, side, vecs : vecs + 1, 0:1] * factor)
            hi, lo = split(came)
            lanes = slice(side * edges, (side + 1) * edges)
            inp[0:vecs, lanes] = hi
            inp[vecs:group_rows, lanes] = lo

    def across(k):
        got = dot(inp[...], same[:, k * pair : (k + 1) * pair])
        return got[0:vecs] + got[vecs:]

    def landed(sl):
        got = dot(inp[...], place[:, sl])
        return got[0:vecs] + got[vecs:]

    def exchange(kind, buf, peer, me, size):
        def one(d):
            return pltpu.make_async_remote_copy(
                src_ref=buf.at[me],
                dst_ref=buf.at[me],
                send_sem=cs.at[kind, d],
                recv_sem=cr.at[kind, d],
                device_id=peer(d),
                device_id_type=MESH,
            )

        return [one(d) for d in range(1, size)]

    def wait_from(kind, buf, me, size, peer, d):
        src = lax.rem(me + size - d, size)
        return pltpu.make_async_remote_copy(
            src_ref=buf.at[src],
            dst_ref=buf.at[src],
            send_sem=cs.at[kind, d],
            recv_sem=cr.at[kind, d],
            device_id=peer(d),
            device_id_type=MESH,
        )

    first = [gather(1), gather(0)]
    pl.semaphore_wait(barrier, size_x + size_y - 2)
    send(0, 1, first[0])
    send(0, 0, first[1])

    for n in range(blocks):
        fetches[n].wait()
        for s in range(stored):
            hi, lo = split(raw[n, s])
            wts[n, 0:block, s * block : (s + 1) * block] = hi
            wts[n, block : 2 * block, s * block : (s + 1) * block] = lo
    wide_live = jnp.broadcast_to(mask[0:1, :], (16, cells)).astype(BF16)
    for t in range(blocks):
        vm[t] = wide_live[:, t * block : (t + 1) * block]
    flags = jnp.concatenate(
        [jnp.full((16, edges), jnp.where(h, 1.0, 0.0).astype(F32), F32) for h in has], axis=1
    ).astype(BF16)
    for sl in chunks:
        deg[:, sl] = dot(flags, pick[sl, :], NT)[0:8]
    for n in range(blocks):
        here = slice(n * block, (n + 1) * block)
        got = dot(
            jnp.concatenate([vm[cols_ref[0, s, 0, n]] for s in range(stored)], axis=1), wts[n], NT
        )
        own = got[0:8, 0:block] + got[0:8, block:]
        deg[:, here] = mask[:, here] * (deg[:, here] + own)
    top = jnp.max(deg[...], axis=1, keepdims=True)
    mxa[me_y] = jnp.broadcast_to(top, (8, 128))
    for c in exchange(0, mxa, peer_y, me_y, size_y):
        c.start()
    local = 2.0 * top[0:1, :]
    local = jnp.where(local > 0.0, local, 1.0)
    shrink = 1.0 / local
    for side in range(sides):
        sbuf[scaled, side, vecs : vecs + 8, :] = jnp.broadcast_to(local, (8, edges))

    def local_z(here, wv):
        rest[:, here] = mask[0:1, here] * (deg[0:1, here] * fa[:, here] - wv) * shrink

    multiply(local_z, block)

    lane = lax.broadcasted_iota(jnp.int32, (128, 128), 1)
    for at in range(0, ends_all, 128):
        side, from_edge = at // edges, at % edges
        ends = edges_ref[0, 0, side : side + 1, from_edge : from_edge + 128]
        col = jnp.transpose(jnp.broadcast_to(ends.astype(F32), (8, 128)))[:, 0:1]
        wide = jnp.broadcast_to(col, (128, 128)).astype(jnp.int32)
        for t in range(0, cells, 128):
            place[at : at + 128, t : t + 128] = jnp.where(wide == lane + t, 1.0, 0.0).astype(BF16)
        for t in range(0, ends_all, 128):
            other = edges_ref[0, 0, t // edges : t // edges + 1, t % edges : t % edges + 128]
            same[at : at + 128, t : t + 128] = jnp.where(wide == other, 1.0, 0.0).astype(BF16)

    for sl in chunks:
        store_parts(sl.start, rest[:, sl])
    ahead = [gather(0), gather(1)]
    receive(0, None)
    for k in (1, 0):
        send(1, k, ahead[k] - across(k) * shrink)
    for sl in chunks:
        z = rest[:, sl] - mask[0:1, sl] * landed(sl) * shrink
        fb[:, sl] = z
        store_parts(sl.start, z)

    for d in range(1, size_y):
        wait_from(0, mxa, me_y, size_y, peer_y, d).wait_recv()
    mxb[me_x] = jnp.max(mxa[...], axis=0)
    for c in exchange(1, mxb, peer_x, me_x, size_x):
        c.start()

    def local_lz(here, wv):
        rest[:, here] = mask[0:1, here] * (deg[0:1, here] * fb[:, here] - wv)

    multiply(local_lz, block)
    for sl in chunks:
        store_parts(sl.start, rest[:, sl])
    ahead = [gather(0), gather(1)]
    receive(1, shrink)
    for d in range(1, size_x):
        wait_from(1, mxb, me_x, size_x, peer_x, d).wait_recv()
    upper = 2.0 * jnp.max(mxb[...], axis=0)[0:1, 0:1]
    lower = LOWER_FRACTION * upper
    half_width = (upper - lower) / 2.0
    centre = (upper + lower) / 2.0
    over = 1.0 / half_width
    ratio = centre * over
    grow = local * over

    def y2_of(lz, z, y0):
        return 2.0 * (grow * (lz * over) - (2.0 * ratio * grow) * z + (ratio * ratio) * y0) - y0

    for k in (1, 0):
        send(2, k, y2_of(ahead[k] - across(k), sent(1, k), sent(0, k)))
    for sl in chunks:
        lz = rest[:, sl] - mask[0:1, sl] * landed(sl)
        z, y0 = fb[:, sl], fa[:, sl]
        y2 = y2_of(lz, z, y0)
        fb[:, sl] = y2
        fa[:, sl] = grow * z - ratio * y0
        store_parts(sl.start, y2)

    twice = 2.0 * over
    previous, current = fa, fb
    for app in (2, 3):

        def local_next(here, wv, previous=previous, current=current):
            y = current[:, here]
            lap = mask[0:1, here] * (deg[0:1, here] * y - wv)
            rest[:, here] = twice * (lap - centre * y) - previous[:, here]

        multiply(local_next, block)
        if app == 2:
            for sl in chunks:
                store_parts(sl.start, rest[:, sl])
            ahead = [gather(0), gather(1)]
        receive(app, None)
        if app == 2:
            for k in (1, 0):
                send(3, k, ahead[k] - twice * across(k))
        for sl in chunks:
            new = rest[:, sl] - mask[0:1, sl] * (twice * landed(sl))
            if app == 2:
                previous[:, sl] = new
            store_parts(sl.start, new)
        previous, current = current, previous

    both = parts_at(0, cells)
    full = dot(both, both, NT)
    gram = full[0:vecs, 0:vecs] + full[0:vecs, vecs:] + full[vecs:, 0:vecs] + full[vecs:, vecs:]
    gram = jnp.concatenate([gram, jnp.zeros((vecs, 128 - vecs), F32)], axis=1)
    owners = vecs // 8
    for p in range(owners):
        gpart[p] = gram[8 * p : 8 * p + 8, :]

    def to_owner(p):
        return pltpu.make_async_remote_copy(
            src_ref=gpart.at[p],
            dst_ref=gr1.at[me_y],
            send_sem=cs.at[2, p],
            recv_sem=cr.at[2, me_y],
            device_id={"gx": me_x, "gy": p},
            device_id_type=MESH,
        )

    def from_member(q):
        return pltpu.make_async_remote_copy(
            src_ref=gr1.at[q],
            dst_ref=gr1.at[q],
            send_sem=cs.at[2, q],
            recv_sem=cr.at[2, q],
            device_id={"gx": me_x, "gy": q},
            device_id_type=MESH,
        )

    def from_owner(p):
        return pltpu.make_async_remote_copy(
            src_ref=gfull.at[p],
            dst_ref=gfull.at[p],
            send_sem=cs.at[4, 0],
            recv_sem=cr.at[4, lax.rem(me_y + size_y - p, size_y)],
            device_id={"gx": me_x, "gy": p},
            device_id_type=MESH,
        )

    for p in range(owners):

        @pl.when(me_y != p)
        def _(p=p):
            to_owner(p).start()

    @pl.when(me_y < owners)
    def _():
        gr1[me_y] = gpart[me_y]
        for q in range(size_y):

            @pl.when(me_y != q)
            def _(q=q):
                from_member(q).wait_recv()

        gr2[me_x] = jnp.sum(gr1[...], axis=0)
        for c in exchange(3, gr2, peer_x, me_x, size_x):
            c.start()
        for d in range(1, size_x):
            wait_from(3, gr2, me_x, size_x, peer_x, d).wait_recv()
        gfull[me_y] = jnp.sum(gr2[...], axis=0)
        for c in exchange(4, gfull, peer_y, me_y, size_y):
            c.start()

    for app in range(4):
        for side in range(sides):

            @pl.when(has[side])
            def _(app=app, side=side):
                halo(app, side, facing[side]).wait_send()

    for c in exchange(0, mxa, peer_y, me_y, size_y) + exchange(1, mxb, peer_x, me_x, size_x):
        c.wait_send()
    for p in range(owners):

        @pl.when(me_y != p)
        def _(p=p):
            to_owner(p).wait_send()

    for p in range(owners):

        @pl.when(me_y != p)
        def _(p=p):
            from_owner(p).wait_recv()

    @pl.when(me_y < owners)
    def _():
        for c in exchange(3, gr2, peer_x, me_x, size_x) + exchange(4, gfull, peer_y, me_y, size_y):
            c.wait_send()


def finish_kernel(scale, gram_ref, parts_ref, out_ref, work, elem, inv):
    vecs = out_ref.shape[2]

    @pl.when(pl.program_id(0) == 0)
    def _():
        work[...] = gram_ref[...]
        inverse_factor(work, elem, inv, scale, vecs)

    hi, lo = split(inv[...])
    hi, lo = hi[:, 0:vecs], lo[:, 0:vecs]
    left = jnp.concatenate(
        [jnp.concatenate([hi, hi], axis=1), jnp.concatenate([lo, lo], axis=1)], axis=0
    )
    right = jnp.concatenate([parts_ref[t] for t in range(parts_ref.shape[0])], axis=1)
    got = dot(left, right)
    out_ref[0, 0] = got[0:vecs] + got[vecs:]


def per_device(size_x, size_y, basis, block_vals, block_cols, edge_rows, live_counts):
    blocks, stored, block = block_vals.shape[2:5]
    vecs, cells = basis.shape[2:]
    sides, edges = edge_rows.shape[2:]
    ends = sides * edges
    vmem = pltpu.VMEM
    field = vmem((vecs, cells), F32)
    scratch = [
        vmem((blocks, stored, block, block), F32),
        vmem((blocks, 2 * block, stored * block), BF16),
        vmem((cells, ends), BF16),
        vmem((ends, cells), BF16),
        vmem((ends, ends), BF16),
        vmem((blocks, 16, block), BF16),
        vmem((2 * vecs, ends), BF16),
        field,
        field,
        field,
        vmem((8, cells), F32),
        vmem((8, cells), F32),
        vmem((4, sides, vecs + 8, edges), F32),
        vmem((4, sides, vecs + 8, edges), F32),
        vmem((size_y, 8, 128), F32),
        vmem((size_x, 8, 128), F32),
        vmem((vecs // 8, 8, 128), F32),
        vmem((size_y, 8, 128), F32),
        vmem((size_x, 8, 128), F32),
        pltpu.SemaphoreType.DMA((blocks,)),
        pltpu.SemaphoreType.DMA((4, sides)),
        pltpu.SemaphoreType.DMA((4, sides)),
        pltpu.SemaphoreType.DMA((5, max(size_x, size_y))),
        pltpu.SemaphoreType.DMA((5, max(size_x, size_y))),
    ]
    in_vmem = pl.BlockSpec(memory_space=vmem)
    in_smem = pl.BlockSpec(memory_space=pltpu.SMEM)
    parts, gram = pl.pallas_call(
        lambda *refs: filter_kernel(size_x, size_y, *refs),
        out_shape=[
            jax.ShapeDtypeStruct((blocks, 2 * vecs, block), BF16),
            jax.ShapeDtypeStruct((vecs // 8, 8, 128), F32),
        ],
        in_specs=[in_smem, in_smem, in_vmem, in_vmem, pl.BlockSpec(memory_space=pl.ANY)],
        out_specs=[in_vmem, in_vmem],
        scratch_shapes=scratch,
        compiler_params=pltpu.CompilerParams(
            collective_id=0, has_side_effects=True, vmem_limit_bytes=60 * 2**20
        ),
        name="filter_and_gram",
    )(live_counts, jnp.transpose(block_cols, (0, 3, 1, 2)), basis, edge_rows, block_vals)
    steps = 4
    return pl.pallas_call(
        lambda *refs: finish_kernel(math.sqrt(cells * size_x * size_y), *refs),
        out_shape=jax.ShapeDtypeStruct(basis.shape, F32),
        grid=(steps,),
        in_specs=[
            pl.BlockSpec(gram.shape, lambda i: (0, 0, 0)),
            pl.BlockSpec((blocks // steps, 2 * vecs, block), lambda i: (i, 0, 0)),
        ],
        out_specs=pl.BlockSpec((1, 1, vecs, cells // steps), lambda i: (0, 0, 0, i)),
        scratch_shapes=[
            vmem(gram.shape, F32),
            vmem((8, 8, 128), F32),
            vmem((vecs, 128), F32),
        ],
        compiler_params=pltpu.CompilerParams(vmem_limit_bytes=60 * 2**20),
        name="factor_and_encode",
    )(gram, parts)


def solution(mesh):
    size_x, size_y = mesh.shape["gx"], mesh.shape["gy"]
    in_specs = (
        P("gx", "gy", None, None),
        P("gx", "gy", None, None, None, None),
        P("gx", "gy", None, None),
        P("gx", "gy", None, None),
        P("gx", "gy"),
    )
    out_specs = P("gx", "gy", None, None)
    return jax.shard_map(
        lambda *args: per_device(size_x, size_y, *args),
        mesh=mesh,
        in_specs=in_specs,
        out_specs=out_specs,
        check_vma=False,
    )
```

```python
import math

import jax
import jax.numpy as jnp
from jax import lax
from jax.experimental import pallas as pl
from jax.experimental.pallas import tpu as pltpu
from jax.sharding import PartitionSpec as P

LOWER_FRACTION = 0.125
MESH = pl.DeviceIdType.MESH
F32 = jnp.float32
BF16 = jnp.bfloat16
NN = (((1,), (0,)), ((), ()))
NT = (((1,), (1,)), ((), ()))


def dot(a, b, dims=NN):
    return lax.dot_general(a, b, dims, preferred_element_type=F32)


def split(x):
    hi = x.astype(BF16)
    lo = (x - hi.astype(F32)).astype(BF16)
    return hi, lo


def inverse_factor(gram_ref, elem_ref, out_ref, scale, rows):
    blocks = rows // 8
    lane = lax.broadcasted_iota(jnp.int32, (8, 128), 1)

    def across(col):
        return jnp.broadcast_to(col, (8, 128))

    for b in range(blocks):
        first = 8 * b
        cols = {}
        for i in range(b, blocks):
            tile = gram_ref[i]
            cols[i] = [across(tile[:, first + k : first + k + 1]) for k in range(8)]
        for k in range(8):
            elem_ref[k] = cols[b][k]
        a = {
            (i, k): across(elem_ref[k, i : i + 1, :]) for k in range(8) for i in range(k, 8)
        }
        inside = (lane >= first) & (lane < first + 8)
        reduced = []
        for k in range(8):
            row = across(gram_ref[b, k : k + 1, :])
            reduced.append(jnp.where(inside, jnp.where(lane == first + k, 1.0, 0.0), row))
        inv = []
        low = {}
        for k in range(8):
            inv.append(1.0 / a[k, k])
            for i in range(k + 1, 8):
                low[i, k] = a[i, k] * inv[k]
                for j in range(k + 1, i + 1):
                    a[i, j] = a[i, j] - low[i, k] * a[j, k]
                reduced[i] = reduced[i] - low[i, k] * reduced[k]
        for i in range(b + 1, blocks):
            u = cols[i]
            for k in range(8):
                for j in range(k + 1, 8):
                    u[j] = u[j] - low[j, k] * u[k]
            tile = jnp.where(inside, 0.0, gram_ref[i])
            for k in range(8):
                tile = tile - (u[k] * inv[k]) * reduced[k]
            gram_ref[i] = tile
        for k in range(8):
            row = jnp.where(lane <= first + k, reduced[k], 0.0) * (lax.rsqrt(a[k, k]) * scale)
            out_ref[first + k : first + k + 1, :] = row[0:1, :]


def far_first(size):
    return sorted(range(1, size), key=lambda d: -min(d, size - d))


def filter_kernel(
    size_x,
    size_y,
    live_ref,
    cols_ref,
    basis_ref,
    edges_ref,
    vals_ref,
    parts_ref,
    gfull,
    vp,
    rp,
    raw,
    wts,
    pick,
    place,
    same,
    vm,
    inp,
    fa,
    fb,
    rest,
    deg,
    mask,
    sbuf,
    rbuf,
    mxa,
    mxb,
    gpart,
    gr1,
    gr2,
    wsem,
    psem,
    hs,
    hr,
    cs,
    cr,
):
    me_x = lax.axis_index("gx")
    me_y = lax.axis_index("gy")
    stored, blocks = cols_ref.shape[1], cols_ref.shape[3]
    block = vals_ref.shape[-1]
    vecs, cells = basis_ref.shape[2], basis_ref.shape[3]
    sides, edges = edges_ref.shape[2], edges_ref.shape[3]
    ends_all = sides * edges
    group_rows = 2 * vecs

    def peer_x(d):
        return {"gx": lax.rem(me_x + d, size_x), "gy": me_y}

    def peer_y(d):
        return {"gx": me_x, "gy": lax.rem(me_y + d, size_y)}

    barrier = pltpu.get_barrier_semaphore()
    for d in range(1, size_x):
        pl.semaphore_signal(barrier, inc=1, device_id=peer_x(d), device_id_type=MESH)
    for d in range(1, size_y):
        pl.semaphore_signal(barrier, inc=1, device_id=peer_y(d), device_id_type=MESH)

    fetches = [
        pltpu.make_async_copy(vals_ref.at[0, 0, n], raw.at[n], wsem.at[n]) for n in range(blocks)
    ]
    for f in fetches:
        f.start()

    has = [me_x > 0, me_x < size_x - 1, me_y > 0, me_y < size_y - 1]
    target = [
        {"gx": me_x - 1, "gy": me_y},
        {"gx": me_x + 1, "gy": me_y},
        {"gx": me_x, "gy": me_y - 1},
        {"gx": me_x, "gy": me_y + 1},
    ]
    facing = [1, 0, 3, 2]
    scaled = 1

    def halo(app, side, into):
        rows = vecs + 8 if app == scaled else vecs
        return pltpu.make_async_remote_copy(
            src_ref=sbuf.at[app, side, pl.ds(0, rows)],
            dst_ref=rbuf.at[app, into, pl.ds(0, rows)],
            send_sem=hs.at[app, side],
            recv_sem=hr.at[app, into],
            device_id=target[side],
            device_id_type=MESH,
        )

    for side in range(sides):

        @pl.when(jnp.logical_not(has[side]))
        def _(side=side):
            for app in range(4):
                rbuf[app, side] = jnp.zeros((vecs + 8, edges), F32)

    lane_id = lax.broadcasted_iota(jnp.int32, (8, cells), 1)
    mask[...] = jnp.where(lane_id < live_ref[0, 0], 1.0, 0.0)

    def store_parts(begin, x, into=vp):
        hi, lo = split(x)
        for t in range(x.shape[1] // block):
            lanes = slice(t * block, (t + 1) * block)
            into[begin // block + t, 0:vecs, :] = hi[:, lanes]
            into[begin // block + t, vecs:group_rows, :] = lo[:, lanes]

    def all_parts(src):
        return jnp.concatenate([src[t] for t in range(blocks)], axis=1)

    start = basis_ref[0, 0] * mask[0:1, :]
    fa[...] = start
    store_parts(0, start)

    step = 128

    @pl.loop(0, cells // step)
    def _(t):
        base = pl.multiple_of(t * step, step)
        cell = lax.broadcasted_iota(jnp.int32, (step, edges), 0) + base
        for side in range(sides):
            ends = edges_ref[0, 0, side : side + 1, :]
            pick[pl.ds(base, step), side * edges : (side + 1) * edges] = jnp.where(
                cell == ends, 1.0, 0.0
            ).astype(BF16)

    chunk = 512
    chunks = [slice(q * chunk, (q + 1) * chunk) for q in range(cells // chunk)]
    pair = 2 * edges

    def gather(k, src):
        got = dot(all_parts(src), pick[:, k * pair : (k + 1) * pair])
        return got[0:vecs] + got[vecs:]

    def send(app, k, values):
        for i in range(2):
            sbuf[app, 2 * k + i, 0:vecs, :] = values[:, i * edges : (i + 1) * edges]
        for i in range(2):

            @pl.when(has[2 * k + i])
            def _(i=i):
                halo(app, 2 * k + i, facing[2 * k + i]).start()

    def sent(app, k):
        return jnp.concatenate([sbuf[app, 2 * k, 0:vecs, :], sbuf[app, 2 * k + 1, 0:vecs, :]], axis=1)

    def multiply(use, width):
        for n in range(blocks):
            got = dot(
                jnp.concatenate([vp[cols_ref[0, s, 0, n]] for s in range(stored)], axis=1),
                wts[n],
                NT,
            )
            use(
                slice(n * block, (n + 1) * block),
                got[0:vecs, 0:width] + got[vecs:, 0:width] + got[0:vecs, width:],
            )

    def receive(app, factor):
        for side in range(sides):

            @pl.when(has[side])
            def _(side=side):
                halo(app, side, side).wait_recv()

        for side in range(sides):
            came = rbuf[app, side, 0:vecs, :]
            if factor is not None:
                came = came * (rbuf[app, side, vecs : vecs + 1, 0:1] * factor)
            hi, lo = split(came)
            lanes = slice(side * edges, (side + 1) * edges)
            inp[0:vecs, lanes] = hi
            inp[vecs:group_rows, lanes] = lo

    def across(k):
        got = dot(inp[...], same[:, k * pair : (k + 1) * pair])
        return got[0:vecs] + got[vecs:]

    def landed(sl):
        got = dot(inp[...], place[:, sl])
        return got[0:vecs] + got[vecs:]

    def exchange(kind, buf, peer, me, size):
        def one(d):
            return pltpu.make_async_remote_copy(
                src_ref=buf.at[me],
                dst_ref=buf.at[me],
                send_sem=cs.at[kind, d],
                recv_sem=cr.at[kind, d],
                device_id=peer(d),
                device_id_type=MESH,
            )

        return [one(d) for d in far_first(size)]

    def wait_from(kind, buf, me, size, peer, d):
        src = lax.rem(me + size - d, size)
        return pltpu.make_async_remote_copy(
            src_ref=buf.at[src],
            dst_ref=buf.at[src],
            send_sem=cs.at[kind, d],
            recv_sem=cr.at[kind, d],
            device_id=peer(d),
            device_id_type=MESH,
        )

    ahead = gather(1, vp)
    pl.semaphore_wait(barrier, size_x + size_y - 2)
    send(0, 1, ahead)
    send(0, 0, gather(0, vp))

    lane = lax.broadcasted_iota(jnp.int32, (128, 128), 1)

    def down(at):
        side, from_edge = at // edges, at % edges
        ends = edges_ref[0, 0, side : side + 1, from_edge : from_edge + 128]
        col = jnp.transpose(jnp.broadcast_to(ends.astype(F32), (8, 128)))[:, 0:1]
        return jnp.broadcast_to(col, (128, 128)).astype(jnp.int32)

    counts = [jnp.zeros((8, 128), F32) for _ in range(cells // 128)]
    for at in range(0, ends_all, 128):
        wide = down(at)
        flag = jnp.where(has[at // edges], 1.0, 0.0).astype(F32)
        for t in range(cells // 128):
            hit = jnp.where(wide == lane + t * 128, 1.0, 0.0)
            place[at : at + 128, t * 128 : (t + 1) * 128] = hit.astype(BF16)
            counts[t] = counts[t] + flag * jnp.sum(hit.reshape(16, 8, 128), axis=0)
    for t in range(cells // 128):
        deg[:, t * 128 : (t + 1) * 128] = jnp.broadcast_to(
            jnp.sum(counts[t], axis=0, keepdims=True), (8, 128)
        )

    for t in range(blocks):
        vm[t] = mask[:, t * block : (t + 1) * block]
    ones = jnp.ones((16, block), BF16)
    for n in range(blocks):
        fetches[n].wait()
        heavy = jnp.zeros((block, block), F32)
        for s in range(stored):
            w = raw[n, s]
            hi, lo = split(w)
            wts[n, 0:block, s * block : (s + 1) * block] = hi
            wts[n, block : 2 * block, s * block : (s + 1) * block] = lo
            heavy = heavy + w * vm[cols_ref[0, s, 0, n]][0:1, :]
        here = slice(n * block, (n + 1) * block)
        got = dot(ones, jnp.concatenate(split(heavy), axis=0), NT)
        own = got[0:8, 0:block] + got[0:8, block:]
        deg[:, here] = mask[:, here] * (deg[:, here] + own)
    top = jnp.max(deg[...], axis=1, keepdims=True)
    mxa[me_y] = jnp.broadcast_to(top, (8, 128))
    for c in exchange(0, mxa, peer_y, me_y, size_y):
        c.start()
    local = 2.0 * top[0:1, :]
    local = jnp.where(local > 0.0, local, 1.0)
    shrink = 1.0 / local
    for side in range(sides):
        sbuf[scaled, side, vecs : vecs + 8, :] = jnp.broadcast_to(local, (8, edges))

    def keep(here, x, for_edges=True):
        rest[:, here] = x
        if for_edges:
            store_parts(here.start, x, rp)

    def local_z(here, wv):
        keep(here, mask[0:1, here] * (deg[0:1, here] * fa[:, here] - wv) * shrink)

    multiply(local_z, block)

    for at in range(0, ends_all, 128):
        wide = down(at)
        for t in range(0, ends_all, 128):
            other = edges_ref[0, 0, t // edges : t // edges + 1, t % edges : t % edges + 128]
            same[at : at + 128, t : t + 128] = jnp.where(wide == other, 1.0, 0.0).astype(BF16)

    ahead = [gather(0, rp), gather(1, rp)]
    receive(0, None)
    for k in (1, 0):
        send(1, k, ahead[k] - across(k) * shrink)
    for d in range(1, size_y):
        wait_from(0, mxa, me_y, size_y, peer_y, d).wait_recv()
    mxb[me_x] = jnp.max(mxa[...], axis=0)
    for c in exchange(1, mxb, peer_x, me_x, size_x):
        c.start()
    for sl in chunks:
        z = rest[:, sl] - mask[0:1, sl] * landed(sl) * shrink
        fb[:, sl] = z
        store_parts(sl.start, z)

    def local_lz(here, wv):
        keep(here, mask[0:1, here] * (deg[0:1, here] * fb[:, here] - wv))

    multiply(local_lz, block)
    ahead = [gather(0, rp), gather(1, rp)]
    receive(1, shrink)
    for d in range(1, size_x):
        wait_from(1, mxb, me_x, size_x, peer_x, d).wait_recv()
    upper = 2.0 * jnp.max(mxb[...], axis=0)[0:1, 0:1]
    lower = LOWER_FRACTION * upper
    half_width = (upper - lower) / 2.0
    centre = (upper + lower) / 2.0
    over = 1.0 / half_width
    ratio = centre * over
    grow = local * over

    def y2_of(lz, z, y0):
        return 2.0 * (grow * (lz * over) - (2.0 * ratio * grow) * z + (ratio * ratio) * y0) - y0

    for k in (1, 0):
        send(2, k, y2_of(ahead[k] - across(k), sent(1, k), sent(0, k)))
    for sl in chunks:
        lz = rest[:, sl] - mask[0:1, sl] * landed(sl)
        z, y0 = fb[:, sl], fa[:, sl]
        y2 = y2_of(lz, z, y0)
        fb[:, sl] = y2
        fa[:, sl] = grow * z - ratio * y0
        store_parts(sl.start, y2)

    twice = 2.0 * over
    previous, current = fa, fb
    for app in (2, 3):

        def local_next(here, wv, app=app, previous=previous, current=current):
            y = current[:, here]
            lap = mask[0:1, here] * (deg[0:1, here] * y - wv)
            keep(here, twice * (lap - centre * y) - previous[:, here], app == 2)

        multiply(local_next, block)
        if app == 2:
            ahead = [gather(0, rp), gather(1, rp)]
        receive(app, None)
        if app == 2:
            for k in (1, 0):
                send(3, k, ahead[k] - twice * across(k))
        for sl in chunks:
            new = rest[:, sl] - mask[0:1, sl] * (twice * landed(sl))
            if app == 2:
                previous[:, sl] = new
            store_parts(sl.start, new)
        previous, current = current, previous

    filtered = pltpu.make_async_copy(vp, parts_ref, psem)
    filtered.start()
    both = all_parts(vp)
    full = dot(both, both, NT)
    gram = full[0:vecs, 0:vecs] + full[0:vecs, vecs:] + full[vecs:, 0:vecs] + full[vecs:, vecs:]
    gram = jnp.concatenate([gram, jnp.zeros((vecs, 128 - vecs), F32)], axis=1)
    owners = vecs // 8
    for p in range(owners):
        gpart[p] = gram[8 * p : 8 * p + 8, :]

    def to_owner(p):
        return pltpu.make_async_remote_copy(
            src_ref=gpart.at[p],
            dst_ref=gr1.at[me_y],
            send_sem=cs.at[2, p],
            recv_sem=cr.at[2, me_y],
            device_id={"gx": me_x, "gy": p},
            device_id_type=MESH,
        )

    def from_member(q):
        return pltpu.make_async_remote_copy(
            src_ref=gr1.at[q],
            dst_ref=gr1.at[q],
            send_sem=cs.at[2, q],
            recv_sem=cr.at[2, q],
            device_id={"gx": me_x, "gy": q},
            device_id_type=MESH,
        )

    def from_owner(p):
        return pltpu.make_async_remote_copy(
            src_ref=gfull.at[p],
            dst_ref=gfull.at[p],
            send_sem=cs.at[4, 0],
            recv_sem=cr.at[4, lax.rem(me_y + size_y - p, size_y)],
            device_id={"gx": me_x, "gy": p},
            device_id_type=MESH,
        )

    for p in range(owners):

        @pl.when(me_y != p)
        def _(p=p):
            to_owner(p).start()

    @pl.when(me_y < owners)
    def _():
        gr1[me_y] = gpart[me_y]
        for q in range(size_y):

            @pl.when(me_y != q)
            def _(q=q):
                from_member(q).wait_recv()

        gr2[me_x] = jnp.sum(gr1[...], axis=0)
        for c in exchange(3, gr2, peer_x, me_x, size_x):
            c.start()
        for d in range(1, size_x):
            wait_from(3, gr2, me_x, size_x, peer_x, d).wait_recv()
        gfull[me_y] = jnp.sum(gr2[...], axis=0)
        for c in exchange(4, gfull, peer_y, me_y, size_y):
            c.start()

    for app in range(4):
        for side in range(sides):

            @pl.when(has[side])
            def _(app=app, side=side):
                halo(app, side, facing[side]).wait_send()

    for c in exchange(0, mxa, peer_y, me_y, size_y) + exchange(1, mxb, peer_x, me_x, size_x):
        c.wait_send()
    for p in range(owners):

        @pl.when(me_y != p)
        def _(p=p):
            to_owner(p).wait_send()

    for p in range(owners):

        @pl.when(me_y != p)
        def _(p=p):
            from_owner(p).wait_recv()

    @pl.when(me_y < owners)
    def _():
        for c in exchange(3, gr2, peer_x, me_x, size_x) + exchange(4, gfull, peer_y, me_y, size_y):
            c.wait_send()

    filtered.wait()


def finish_kernel(scale, gram_ref, parts_ref, out_ref, work, elem, inv, parts, result, psem, osem):
    vecs, cells = out_ref.shape[2:]
    fetch = pltpu.make_async_copy(parts_ref, parts, psem)
    fetch.start()
    work[...] = gram_ref[...]
    inverse_factor(work, elem, inv, scale, vecs)
    hi, lo = split(inv[...])
    hi, lo = hi[:, 0:vecs], lo[:, 0:vecs]
    left = jnp.concatenate(
        [jnp.concatenate([hi, hi], axis=1), jnp.concatenate([lo, lo], axis=1)], axis=0
    )
    fetch.wait()
    blocks, chunks = parts.shape[0], osem.shape[0]
    each, width = blocks // chunks, cells // chunks
    writes = []
    for q in range(chunks):
        got = dot(left, jnp.concatenate([parts[q * each + t] for t in range(each)], axis=1))
        result[q] = got[0:vecs] + got[vecs:]
        writes.append(
            pltpu.make_async_copy(
                result.at[q], out_ref.at[0, 0, :, pl.ds(q * width, width)], osem.at[q]
            )
        )
        writes[q].start()
    for w in writes:
        w.wait()


def per_device(size_x, size_y, basis, block_vals, block_cols, edge_rows, live_counts):
    blocks, stored, block = block_vals.shape[2:5]
    vecs, cells = basis.shape[2:]
    sides, edges = edge_rows.shape[2:]
    ends = sides * edges
    vmem = pltpu.VMEM
    field = vmem((vecs, cells), F32)
    scratch = [
        vmem((blocks, 2 * vecs, block), BF16),
        vmem((blocks, 2 * vecs, block), BF16),
        vmem((blocks, stored, block, block), F32),
        vmem((blocks, 2 * block, stored * block), BF16),
        vmem((cells, ends), BF16),
        vmem((ends, cells), BF16),
        vmem((ends, ends), BF16),
        vmem((blocks, 8, block), F32),
        vmem((2 * vecs, ends), BF16),
        field,
        field,
        field,
        vmem((8, cells), F32),
        vmem((8, cells), F32),
        vmem((4, sides, vecs + 8, edges), F32),
        vmem((4, sides, vecs + 8, edges), F32),
        vmem((size_y, 8, 128), F32),
        vmem((size_x, 8, 128), F32),
        vmem((vecs // 8, 8, 128), F32),
        vmem((size_y, 8, 128), F32),
        vmem((size_x, 8, 128), F32),
        pltpu.SemaphoreType.DMA((blocks,)),
        pltpu.SemaphoreType.DMA,
        pltpu.SemaphoreType.DMA((4, sides)),
        pltpu.SemaphoreType.DMA((4, sides)),
        pltpu.SemaphoreType.DMA((5, max(size_x, size_y))),
        pltpu.SemaphoreType.DMA((5, max(size_x, size_y))),
    ]
    in_vmem = pl.BlockSpec(memory_space=vmem)
    in_smem = pl.BlockSpec(memory_space=pltpu.SMEM)
    parts, gram = pl.pallas_call(
        lambda *refs: filter_kernel(size_x, size_y, *refs),
        out_shape=[
            jax.ShapeDtypeStruct((blocks, 2 * vecs, block), BF16),
            jax.ShapeDtypeStruct((vecs // 8, 8, 128), F32),
        ],
        in_specs=[in_smem, in_smem, in_vmem, in_vmem, pl.BlockSpec(memory_space=pl.ANY)],
        out_specs=[pl.BlockSpec(memory_space=pl.ANY), in_vmem],
        scratch_shapes=scratch,
        compiler_params=pltpu.CompilerParams(
            collective_id=0, has_side_effects=True, vmem_limit_bytes=60 * 2**20
        ),
        name="filter_and_gram",
    )(live_counts, jnp.transpose(block_cols, (0, 3, 1, 2)), basis, edge_rows, block_vals)
    steps = 4
    return pl.pallas_call(
        lambda *refs: finish_kernel(math.sqrt(cells * size_x * size_y), *refs),
        out_shape=jax.ShapeDtypeStruct(basis.shape, F32),
        in_specs=[in_vmem, pl.BlockSpec(memory_space=pl.ANY)],
        out_specs=pl.BlockSpec(memory_space=pl.ANY),
        scratch_shapes=[
            vmem(gram.shape, F32),
            vmem((8, 8, 128), F32),
            vmem((vecs, 128), F32),
            vmem(parts.shape, BF16),
            vmem((steps, vecs, cells // steps), F32),
            pltpu.SemaphoreType.DMA,
            pltpu.SemaphoreType.DMA((steps,)),
        ],
        compiler_params=pltpu.CompilerParams(vmem_limit_bytes=60 * 2**20),
        name="factor_and_encode",
    )(gram, parts)


def solution(mesh):
    size_x, size_y = mesh.shape["gx"], mesh.shape["gy"]
    in_specs = (
        P("gx", "gy", None, None),
        P("gx", "gy", None, None, None, None),
        P("gx", "gy", None, None),
        P("gx", "gy", None, None),
        P("gx", "gy"),
    )
    out_specs = P("gx", "gy", None, None)
    return jax.shard_map(
        lambda *args: per_device(size_x, size_y, *args),
        mesh=mesh,
        in_specs=in_specs,
        out_specs=out_specs,
        check_vma=False,
    )
```

```python
import math

import jax
import jax.numpy as jnp
from jax import lax
from jax.experimental import pallas as pl
from jax.experimental.pallas import tpu as pltpu
from jax.sharding import PartitionSpec as P

LOWER_FRACTION = 0.125
MESH = pl.DeviceIdType.MESH
F32 = jnp.float32
BF16 = jnp.bfloat16
NN = (((1,), (0,)), ((), ()))
NT = (((1,), (1,)), ((), ()))


def dot(a, b, dims=NN):
    return lax.dot_general(a, b, dims, preferred_element_type=F32)


def split(x):
    hi = x.astype(BF16)
    lo = (x - hi.astype(F32)).astype(BF16)
    return hi, lo


def inverse_factor(gram_ref, elem_ref, out_ref, scale, rows):
    blocks = rows // 8
    lane = lax.broadcasted_iota(jnp.int32, (8, 128), 1)

    def across(col):
        return jnp.broadcast_to(col, (8, 128))

    for b in range(blocks):
        first = 8 * b
        cols = {}
        for i in range(b, blocks):
            tile = gram_ref[i]
            cols[i] = [across(tile[:, first + k : first + k + 1]) for k in range(8)]
        for k in range(8):
            elem_ref[k] = cols[b][k]
        a = {
            (i, k): across(elem_ref[k, i : i + 1, :]) for k in range(8) for i in range(k, 8)
        }
        inside = (lane >= first) & (lane < first + 8)
        reduced = []
        for k in range(8):
            row = across(gram_ref[b, k : k + 1, :])
            reduced.append(jnp.where(inside, jnp.where(lane == first + k, 1.0, 0.0), row))
        inv = []
        low = {}
        for k in range(8):
            inv.append(1.0 / a[k, k])
            for i in range(k + 1, 8):
                low[i, k] = a[i, k] * inv[k]
                for j in range(k + 1, i + 1):
                    a[i, j] = a[i, j] - low[i, k] * a[j, k]
                reduced[i] = reduced[i] - low[i, k] * reduced[k]
        for i in range(b + 1, blocks):
            u = cols[i]
            for k in range(8):
                for j in range(k + 1, 8):
                    u[j] = u[j] - low[j, k] * u[k]
            tile = jnp.where(inside, 0.0, gram_ref[i])
            for k in range(8):
                tile = tile - (u[k] * inv[k]) * reduced[k]
            gram_ref[i] = tile
        for k in range(8):
            row = jnp.where(lane <= first + k, reduced[k], 0.0) * (lax.rsqrt(a[k, k]) * scale)
            out_ref[first + k : first + k + 1, :] = row[0:1, :]


def far_first(size):
    return sorted(range(1, size), key=lambda d: -min(d, size - d))


def filter_kernel(
    size_x,
    size_y,
    live_ref,
    cols_ref,
    basis_ref,
    edges_ref,
    vals_ref,
    parts_ref,
    gfull,
    vp,
    rp,
    raw,
    wts,
    pick,
    place,
    same,
    vm,
    inp,
    fa,
    fb,
    rest,
    deg,
    mask,
    sbuf,
    rbuf,
    mxa,
    mxb,
    gpart,
    gr1,
    gr2,
    wsem,
    psem,
    hs,
    hr,
    cs,
    cr,
):
    me_x = lax.axis_index("gx")
    me_y = lax.axis_index("gy")
    stored, blocks = cols_ref.shape[1], cols_ref.shape[3]
    block = vals_ref.shape[-1]
    vecs, cells = basis_ref.shape[2], basis_ref.shape[3]
    sides, edges = edges_ref.shape[2], edges_ref.shape[3]
    ends_all = sides * edges
    group_rows = 2 * vecs

    def peer_x(d):
        return {"gx": lax.rem(me_x + d, size_x), "gy": me_y}

    def peer_y(d):
        return {"gx": me_x, "gy": lax.rem(me_y + d, size_y)}

    fetches = [
        pltpu.make_async_copy(vals_ref.at[0, 0, n], raw.at[n], wsem.at[n]) for n in range(blocks)
    ]
    for f in fetches:
        f.start()

    barrier = pltpu.get_barrier_semaphore()
    for d in range(1, size_x):
        pl.semaphore_signal(barrier, inc=1, device_id=peer_x(d), device_id_type=MESH)
    for d in range(1, size_y):
        pl.semaphore_signal(barrier, inc=1, device_id=peer_y(d), device_id_type=MESH)

    has = [me_x > 0, me_x < size_x - 1, me_y > 0, me_y < size_y - 1]
    target = [
        {"gx": me_x - 1, "gy": me_y},
        {"gx": me_x + 1, "gy": me_y},
        {"gx": me_x, "gy": me_y - 1},
        {"gx": me_x, "gy": me_y + 1},
    ]
    facing = [1, 0, 3, 2]
    scaled = 1

    def halo(app, side, into):
        rows = vecs + 8 if app == scaled else vecs
        return pltpu.make_async_remote_copy(
            src_ref=sbuf.at[app, side, pl.ds(0, rows)],
            dst_ref=rbuf.at[app, into, pl.ds(0, rows)],
            send_sem=hs.at[app, side],
            recv_sem=hr.at[app, into],
            device_id=target[side],
            device_id_type=MESH,
        )

    for side in range(sides):

        @pl.when(jnp.logical_not(has[side]))
        def _(side=side):
            for app in range(4):
                rbuf[app, side] = jnp.zeros((vecs + 8, edges), F32)

    lane_id = lax.broadcasted_iota(jnp.int32, (8, cells), 1)
    mask[...] = jnp.where(lane_id < live_ref[0, 0], 1.0, 0.0)

    def store_parts(begin, x, into=vp):
        hi, lo = split(x)
        for t in range(x.shape[1] // block):
            lanes = slice(t * block, (t + 1) * block)
            into[begin // block + t, 0:vecs, :] = hi[:, lanes]
            into[begin // block + t, vecs:group_rows, :] = lo[:, lanes]

    def all_parts(src):
        return jnp.concatenate([src[t] for t in range(blocks)], axis=1)

    start = basis_ref[0, 0] * mask[0:1, :]
    fa[...] = start
    store_parts(0, start)

    step = 128
    position = lax.broadcasted_iota(jnp.int32, (step, edges), 0).astype(F32).astype(BF16)
    one, none = jnp.ones((step, edges), BF16), jnp.zeros((step, edges), BF16)

    @pl.loop(0, cells // step)
    def _(t):
        base = pl.multiple_of(t * step, step)
        for side in range(sides):
            inside = edges_ref[0, 0, side : side + 1, :] - base
            inside = jnp.where((inside >= 0) & (inside < step), inside, 255)
            key = jnp.broadcast_to(inside.astype(F32), (step, edges)).astype(BF16)
            pick[pl.ds(base, step), side * edges : (side + 1) * edges] = jnp.where(
                position == key, one, none
            )

    chunk = 512
    chunks = [slice(q * chunk, (q + 1) * chunk) for q in range(cells // chunk)]
    pair = 2 * edges

    def gather(k, src):
        got = dot(all_parts(src), pick[:, k * pair : (k + 1) * pair])
        return got[0:vecs] + got[vecs:]

    def send(app, k, values):
        for i in range(2):
            sbuf[app, 2 * k + i, 0:vecs, :] = values[:, i * edges : (i + 1) * edges]
        for i in range(2):

            @pl.when(has[2 * k + i])
            def _(i=i):
                halo(app, 2 * k + i, facing[2 * k + i]).start()

    def sent(app, k):
        return jnp.concatenate([sbuf[app, 2 * k, 0:vecs, :], sbuf[app, 2 * k + 1, 0:vecs, :]], axis=1)

    def multiply(use, width):
        for n in range(blocks):
            got = dot(
                jnp.concatenate([vp[cols_ref[0, s, 0, n]] for s in range(stored)], axis=1),
                wts[n],
                NT,
            )
            use(
                slice(n * block, (n + 1) * block),
                got[0:vecs, 0:width] + got[vecs:, 0:width] + got[0:vecs, width:],
            )

    def receive(app, factor):
        for side in range(sides):

            @pl.when(has[side])
            def _(side=side):
                halo(app, side, side).wait_recv()

        for side in range(sides):
            came = rbuf[app, side, 0:vecs, :]
            if factor is not None:
                came = came * (rbuf[app, side, vecs : vecs + 1, 0:1] * factor)
            hi, lo = split(came)
            lanes = slice(side * edges, (side + 1) * edges)
            inp[0:vecs, lanes] = hi
            inp[vecs:group_rows, lanes] = lo

    def across(k):
        got = dot(inp[...], same[:, k * pair : (k + 1) * pair])
        return got[0:vecs] + got[vecs:]

    def landed(sl):
        got = dot(inp[...], place[:, sl])
        return got[0:vecs] + got[vecs:]

    def exchange(kind, buf, peer, me, size):
        def one(d):
            return pltpu.make_async_remote_copy(
                src_ref=buf.at[me],
                dst_ref=buf.at[me],
                send_sem=cs.at[kind, d],
                recv_sem=cr.at[kind, d],
                device_id=peer(d),
                device_id_type=MESH,
            )

        return [one(d) for d in far_first(size)]

    def wait_from(kind, buf, me, size, peer, d):
        src = lax.rem(me + size - d, size)
        return pltpu.make_async_remote_copy(
            src_ref=buf.at[src],
            dst_ref=buf.at[src],
            send_sem=cs.at[kind, d],
            recv_sem=cr.at[kind, d],
            device_id=peer(d),
            device_id_type=MESH,
        )

    ahead = gather(1, vp)
    pl.semaphore_wait(barrier, size_x + size_y - 2)
    send(0, 1, ahead)
    send(0, 0, gather(0, vp))

    lane = lax.broadcasted_iota(jnp.int32, (128, 128), 1).astype(F32).astype(BF16)
    zero = jnp.zeros((128, 128), BF16)

    def apart(ends):
        high = lax.shift_right_logical(ends, 7)
        return high.astype(F32), (ends - high * 128).astype(F32)

    def down(at):
        side, from_edge = at // edges, at % edges
        ends = edges_ref[0, 0, side : side + 1, from_edge : from_edge + 128]
        wide = [
            jnp.broadcast_to(
                jnp.transpose(jnp.broadcast_to(x, (8, 128)))[:, 0:1], (128, 128)
            ).astype(BF16)
            for x in apart(ends)
        ]
        return wide[0], wide[1], jnp.where(wide[1] == lane, jnp.ones((128, 128), BF16), zero)

    counts = [jnp.zeros((16, 128), F32) for _ in range(cells // 128)]
    for at in range(0, ends_all, 128):
        high, _, spot = down(at)
        flag = jnp.where(has[at // edges], 1.0, 0.0).astype(F32)
        for t in range(cells // 128):
            hit = jnp.where(high == jnp.full((128, 128), t, BF16), spot, zero)
            place[at : at + 128, t * 128 : (t + 1) * 128] = hit
            some = hit[0:16]
            for r in range(16, 128, 16):
                some = some + hit[r : r + 16]
            counts[t] = counts[t] + flag * some.astype(F32)
    for t in range(cells // 128):
        deg[:, t * 128 : (t + 1) * 128] = jnp.broadcast_to(
            jnp.sum(counts[t], axis=0, keepdims=True), (8, 128)
        )

    for t in range(blocks):
        vm[t] = mask[:, t * block : (t + 1) * block]
    ones = jnp.ones((16, block), BF16)
    for n in range(blocks):
        fetches[n].wait()
        heavy = jnp.zeros((block, block), F32)
        for s in range(stored):
            w = raw[n, s]
            hi, lo = split(w)
            wts[n, 0:block, s * block : (s + 1) * block] = hi
            wts[n, block : 2 * block, s * block : (s + 1) * block] = lo
            heavy = heavy + w * vm[cols_ref[0, s, 0, n]][0:1, :]
        here = slice(n * block, (n + 1) * block)
        got = dot(ones, jnp.concatenate(split(heavy), axis=0), NT)
        own = got[0:8, 0:block] + got[0:8, block:]
        deg[:, here] = mask[:, here] * (deg[:, here] + own)
    top = jnp.max(deg[...], axis=1, keepdims=True)
    mxa[me_y] = jnp.broadcast_to(top, (8, 128))
    for c in exchange(0, mxa, peer_y, me_y, size_y):
        c.start()
    local = 2.0 * top[0:1, :]
    local = jnp.where(local > 0.0, local, 1.0)
    shrink = 1.0 / local
    for side in range(sides):
        sbuf[scaled, side, vecs : vecs + 8, :] = jnp.broadcast_to(local, (8, edges))

    def keep(here, x, for_edges=True):
        rest[:, here] = x
        if for_edges:
            store_parts(here.start, x, rp)

    def local_z(here, wv):
        keep(here, mask[0:1, here] * (deg[0:1, here] * fa[:, here] - wv) * shrink)

    multiply(local_z, block)

    for at in range(0, ends_all, 128):
        high, low, _ = down(at)
        for t in range(0, ends_all, 128):
            other = edges_ref[0, 0, t // edges : t // edges + 1, t % edges : t % edges + 128]
            far_high, far_low = (
                jnp.broadcast_to(x, (128, 128)).astype(BF16) for x in apart(other)
            )
            meet = jnp.where(low == far_low, jnp.ones((128, 128), BF16), zero)
            same[at : at + 128, t : t + 128] = jnp.where(high == far_high, meet, zero)

    ahead = [gather(0, rp), gather(1, rp)]
    receive(0, None)
    for k in (1, 0):
        send(1, k, ahead[k] - across(k) * shrink)
    for d in range(1, size_y):
        wait_from(0, mxa, me_y, size_y, peer_y, d).wait_recv()
    mxb[me_x] = jnp.max(mxa[...], axis=0)
    for c in exchange(1, mxb, peer_x, me_x, size_x):
        c.start()
    for sl in chunks:
        z = rest[:, sl] - mask[0:1, sl] * landed(sl) * shrink
        fb[:, sl] = z
        store_parts(sl.start, z)

    def local_lz(here, wv):
        keep(here, mask[0:1, here] * (deg[0:1, here] * fb[:, here] - wv))

    multiply(local_lz, block)
    ahead = [gather(0, rp), gather(1, rp)]
    receive(1, shrink)
    for d in range(1, size_x):
        wait_from(1, mxb, me_x, size_x, peer_x, d).wait_recv()
    upper = 2.0 * jnp.max(mxb[...], axis=0)[0:1, 0:1]
    lower = LOWER_FRACTION * upper
    half_width = (upper - lower) / 2.0
    centre = (upper + lower) / 2.0
    over = 1.0 / half_width
    ratio = centre * over
    grow = local * over

    def y2_of(lz, z, y0):
        return 2.0 * (grow * (lz * over) - (2.0 * ratio * grow) * z + (ratio * ratio) * y0) - y0

    for k in (1, 0):
        send(2, k, y2_of(ahead[k] - across(k), sent(1, k), sent(0, k)))
    for sl in chunks:
        lz = rest[:, sl] - mask[0:1, sl] * landed(sl)
        z, y0 = fb[:, sl], fa[:, sl]
        y2 = y2_of(lz, z, y0)
        fb[:, sl] = y2
        fa[:, sl] = grow * z - ratio * y0
        store_parts(sl.start, y2)

    twice = 2.0 * over
    previous, current = fa, fb
    for app in (2, 3):

        def local_next(here, wv, app=app, previous=previous, current=current):
            y = current[:, here]
            lap = mask[0:1, here] * (deg[0:1, here] * y - wv)
            keep(here, twice * (lap - centre * y) - previous[:, here], app == 2)

        multiply(local_next, block)
        if app == 2:
            ahead = [gather(0, rp), gather(1, rp)]
        receive(app, None)
        if app == 2:
            for k in (1, 0):
                send(3, k, ahead[k] - twice * across(k))
        for sl in chunks:
            new = rest[:, sl] - mask[0:1, sl] * (twice * landed(sl))
            if app == 2:
                previous[:, sl] = new
            store_parts(sl.start, new)
        previous, current = current, previous

    filtered = pltpu.make_async_copy(vp, parts_ref, psem)
    filtered.start()
    both = all_parts(vp)
    full = dot(both, both, NT)
    gram = full[0:vecs, 0:vecs] + full[0:vecs, vecs:] + full[vecs:, 0:vecs] + full[vecs:, vecs:]
    gram = jnp.concatenate([gram, jnp.zeros((vecs, 128 - vecs), F32)], axis=1)
    owners = vecs // 8
    for p in range(owners):
        gpart[p] = gram[8 * p : 8 * p + 8, :]

    def to_owner(p):
        return pltpu.make_async_remote_copy(
            src_ref=gpart.at[p],
            dst_ref=gr1.at[me_y],
            send_sem=cs.at[2, p],
            recv_sem=cr.at[2, me_y],
            device_id={"gx": me_x, "gy": p},
            device_id_type=MESH,
        )

    def from_member(q):
        return pltpu.make_async_remote_copy(
            src_ref=gr1.at[q],
            dst_ref=gr1.at[q],
            send_sem=cs.at[2, q],
            recv_sem=cr.at[2, q],
            device_id={"gx": me_x, "gy": q},
            device_id_type=MESH,
        )

    def from_owner(p):
        return pltpu.make_async_remote_copy(
            src_ref=gfull.at[p],
            dst_ref=gfull.at[p],
            send_sem=cs.at[4, 0],
            recv_sem=cr.at[4, lax.rem(me_y + size_y - p, size_y)],
            device_id={"gx": me_x, "gy": p},
            device_id_type=MESH,
        )

    for p in range(owners):

        @pl.when(me_y != p)
        def _(p=p):
            to_owner(p).start()

    @pl.when(me_y < owners)
    def _():
        gr1[me_y] = gpart[me_y]
        for q in range(size_y):

            @pl.when(me_y != q)
            def _(q=q):
                from_member(q).wait_recv()

        gr2[me_x] = jnp.sum(gr1[...], axis=0)
        for c in exchange(3, gr2, peer_x, me_x, size_x):
            c.start()
        for d in range(1, size_x):
            wait_from(3, gr2, me_x, size_x, peer_x, d).wait_recv()
        gfull[me_y] = jnp.sum(gr2[...], axis=0)
        for c in exchange(4, gfull, peer_y, me_y, size_y):
            c.start()

    for app in range(4):
        for side in range(sides):

            @pl.when(has[side])
            def _(app=app, side=side):
                halo(app, side, facing[side]).wait_send()

    for c in exchange(0, mxa, peer_y, me_y, size_y) + exchange(1, mxb, peer_x, me_x, size_x):
        c.wait_send()
    for p in range(owners):

        @pl.when(me_y != p)
        def _(p=p):
            to_owner(p).wait_send()

    for p in range(owners):

        @pl.when(me_y != p)
        def _(p=p):
            from_owner(p).wait_recv()

    @pl.when(me_y < owners)
    def _():
        for c in exchange(3, gr2, peer_x, me_x, size_x) + exchange(4, gfull, peer_y, me_y, size_y):
            c.wait_send()

    filtered.wait()


def finish_kernel(scale, gram_ref, parts_ref, out_ref, work, elem, inv, parts, result, psem, osem):
    vecs, cells = out_ref.shape[2:]
    fetch = pltpu.make_async_copy(parts_ref, parts, psem)
    fetch.start()
    work[...] = gram_ref[...]
    inverse_factor(work, elem, inv, scale, vecs)
    hi, lo = split(inv[...])
    hi, lo = hi[:, 0:vecs], lo[:, 0:vecs]
    left = jnp.concatenate(
        [jnp.concatenate([hi, hi], axis=1), jnp.concatenate([lo, lo], axis=1)], axis=0
    )
    fetch.wait()
    blocks, chunks = parts.shape[0], osem.shape[0]
    each, width = blocks // chunks, cells // chunks
    writes = []
    for q in range(chunks):
        got = dot(left, jnp.concatenate([parts[q * each + t] for t in range(each)], axis=1))
        result[q] = got[0:vecs] + got[vecs:]
        writes.append(
            pltpu.make_async_copy(
                result.at[q], out_ref.at[0, 0, :, pl.ds(q * width, width)], osem.at[q]
            )
        )
        writes[q].start()
    for w in writes:
        w.wait()


def per_device(size_x, size_y, basis, block_vals, block_cols, edge_rows, live_counts):
    blocks, stored, block = block_vals.shape[2:5]
    vecs, cells = basis.shape[2:]
    sides, edges = edge_rows.shape[2:]
    ends = sides * edges
    vmem = pltpu.VMEM
    field = vmem((vecs, cells), F32)
    scratch = [
        vmem((blocks, 2 * vecs, block), BF16),
        vmem((blocks, 2 * vecs, block), BF16),
        vmem((blocks, stored, block, block), F32),
        vmem((blocks, 2 * block, stored * block), BF16),
        vmem((cells, ends), BF16),
        vmem((ends, cells), BF16),
        vmem((ends, ends), BF16),
        vmem((blocks, 8, block), F32),
        vmem((2 * vecs, ends), BF16),
        field,
        field,
        field,
        vmem((8, cells), F32),
        vmem((8, cells), F32),
        vmem((4, sides, vecs + 8, edges), F32),
        vmem((4, sides, vecs + 8, edges), F32),
        vmem((size_y, 8, 128), F32),
        vmem((size_x, 8, 128), F32),
        vmem((vecs // 8, 8, 128), F32),
        vmem((size_y, 8, 128), F32),
        vmem((size_x, 8, 128), F32),
        pltpu.SemaphoreType.DMA((blocks,)),
        pltpu.SemaphoreType.DMA,
        pltpu.SemaphoreType.DMA((4, sides)),
        pltpu.SemaphoreType.DMA((4, sides)),
        pltpu.SemaphoreType.DMA((5, max(size_x, size_y))),
        pltpu.SemaphoreType.DMA((5, max(size_x, size_y))),
    ]
    in_vmem = pl.BlockSpec(memory_space=vmem)
    in_smem = pl.BlockSpec(memory_space=pltpu.SMEM)
    parts, gram = pl.pallas_call(
        lambda *refs: filter_kernel(size_x, size_y, *refs),
        out_shape=[
            jax.ShapeDtypeStruct((blocks, 2 * vecs, block), BF16),
            jax.ShapeDtypeStruct((vecs // 8, 8, 128), F32),
        ],
        in_specs=[in_smem, in_smem, in_vmem, in_vmem, pl.BlockSpec(memory_space=pl.ANY)],
        out_specs=[pl.BlockSpec(memory_space=pl.ANY), in_vmem],
        scratch_shapes=scratch,
        compiler_params=pltpu.CompilerParams(
            collective_id=0, has_side_effects=True, vmem_limit_bytes=60 * 2**20
        ),
        name="filter_and_gram",
    )(live_counts, jnp.transpose(block_cols, (0, 3, 1, 2)), basis, edge_rows, block_vals)
    steps = 4
    return pl.pallas_call(
        lambda *refs: finish_kernel(math.sqrt(cells * size_x * size_y), *refs),
        out_shape=jax.ShapeDtypeStruct(basis.shape, F32),
        in_specs=[in_vmem, pl.BlockSpec(memory_space=pl.ANY)],
        out_specs=pl.BlockSpec(memory_space=pl.ANY),
        scratch_shapes=[
            vmem(gram.shape, F32),
            vmem((8, 8, 128), F32),
            vmem((vecs, 128), F32),
            vmem(parts.shape, BF16),
            vmem((steps, vecs, cells // steps), F32),
            pltpu.SemaphoreType.DMA,
            pltpu.SemaphoreType.DMA((steps,)),
        ],
        compiler_params=pltpu.CompilerParams(vmem_limit_bytes=60 * 2**20),
        name="factor_and_encode",
    )(gram, parts)


def solution(mesh):
    size_x, size_y = mesh.shape["gx"], mesh.shape["gy"]
    in_specs = (
        P("gx", "gy", None, None),
        P("gx", "gy", None, None, None, None),
        P("gx", "gy", None, None),
        P("gx", "gy", None, None),
        P("gx", "gy"),
    )
    out_specs = P("gx", "gy", None, None)
    return jax.shard_map(
        lambda *args: per_device(size_x, size_y, *args),
        mesh=mesh,
        in_specs=in_specs,
        out_specs=out_specs,
        check_vma=False,
    )
```

```python
import math

import jax
import jax.numpy as jnp
from jax import lax
from jax.experimental import pallas as pl
from jax.experimental.pallas import tpu as pltpu
from jax.sharding import PartitionSpec as P

LOWER_FRACTION = 0.125
MESH = pl.DeviceIdType.MESH
F32 = jnp.float32
BF16 = jnp.bfloat16
NN = (((1,), (0,)), ((), ()))
NT = (((1,), (1,)), ((), ()))


def dot(a, b, dims=NN):
    return lax.dot_general(a, b, dims, preferred_element_type=F32)


def split(x):
    hi = x.astype(BF16)
    lo = (x - hi.astype(F32)).astype(BF16)
    return hi, lo


def inverse_factor(gram_ref, elem_ref, out_ref, scale, rows):
    blocks = rows // 8
    lane = lax.broadcasted_iota(jnp.int32, (8, 128), 1)

    def across(col):
        return jnp.broadcast_to(col, (8, 128))

    for b in range(blocks):
        first = 8 * b
        cols = {}
        for i in range(b, blocks):
            tile = gram_ref[i]
            cols[i] = [across(tile[:, first + k : first + k + 1]) for k in range(8)]
        for k in range(8):
            elem_ref[k] = cols[b][k]
        a = {
            (i, k): across(elem_ref[k, i : i + 1, :]) for k in range(8) for i in range(k, 8)
        }
        inside = (lane >= first) & (lane < first + 8)
        reduced = []
        for k in range(8):
            row = across(gram_ref[b, k : k + 1, :])
            reduced.append(jnp.where(inside, jnp.where(lane == first + k, 1.0, 0.0), row))
        inv = []
        low = {}
        for k in range(8):
            inv.append(1.0 / a[k, k])
            for i in range(k + 1, 8):
                low[i, k] = a[i, k] * inv[k]
                for j in range(k + 1, i + 1):
                    a[i, j] = a[i, j] - low[i, k] * a[j, k]
                reduced[i] = reduced[i] - low[i, k] * reduced[k]
        for i in range(b + 1, blocks):
            u = cols[i]
            for k in range(8):
                for j in range(k + 1, 8):
                    u[j] = u[j] - low[j, k] * u[k]
            tile = jnp.where(inside, 0.0, gram_ref[i])
            for k in range(8):
                tile = tile - (u[k] * inv[k]) * reduced[k]
            gram_ref[i] = tile
        for k in range(8):
            row = jnp.where(lane <= first + k, reduced[k], 0.0) * (lax.rsqrt(a[k, k]) * scale)
            out_ref[first + k : first + k + 1, :] = row[0:1, :]


def far_first(size):
    return sorted(range(1, size), key=lambda d: -min(d, size - d))


def filter_kernel(
    size_x,
    size_y,
    live_ref,
    cols_ref,
    basis_ref,
    edges_ref,
    vals_ref,
    parts_ref,
    gfull,
    vp,
    rp,
    raw,
    wts,
    pick,
    place,
    same,
    vm,
    inp,
    fa,
    fb,
    rest,
    deg,
    mask,
    sbuf,
    rbuf,
    mxa,
    mxb,
    gpart,
    gr1,
    gr2,
    wsem,
    psem,
    bsem,
    hs,
    hr,
    cs,
    cr,
):
    me_x = lax.axis_index("gx")
    me_y = lax.axis_index("gy")
    stored, blocks = cols_ref.shape[1], cols_ref.shape[3]
    block = vals_ref.shape[-1]
    vecs, cells = basis_ref.shape[2], basis_ref.shape[3]
    sides, edges = edges_ref.shape[2], edges_ref.shape[3]
    ends_all = sides * edges
    group_rows = 2 * vecs

    def peer_x(d):
        return {"gx": lax.rem(me_x + d, size_x), "gy": me_y}

    def peer_y(d):
        return {"gx": me_x, "gy": lax.rem(me_y + d, size_y)}

    load = pltpu.make_async_copy(basis_ref.at[0, 0], rest, bsem)
    load.start()
    fetches = [
        pltpu.make_async_copy(vals_ref.at[0, 0, n], raw.at[n], wsem.at[n]) for n in range(blocks)
    ]
    for f in fetches:
        f.start()

    barrier = pltpu.get_barrier_semaphore()
    for d in range(1, size_x):
        pl.semaphore_signal(barrier, inc=1, device_id=peer_x(d), device_id_type=MESH)
    for d in range(1, size_y):
        pl.semaphore_signal(barrier, inc=1, device_id=peer_y(d), device_id_type=MESH)

    has = [me_x > 0, me_x < size_x - 1, me_y > 0, me_y < size_y - 1]
    target = [
        {"gx": me_x - 1, "gy": me_y},
        {"gx": me_x + 1, "gy": me_y},
        {"gx": me_x, "gy": me_y - 1},
        {"gx": me_x, "gy": me_y + 1},
    ]
    facing = [1, 0, 3, 2]
    scaled = 1

    def halo(app, side, into):
        rows = vecs + 8 if app == scaled else vecs
        return pltpu.make_async_remote_copy(
            src_ref=sbuf.at[app, side, pl.ds(0, rows)],
            dst_ref=rbuf.at[app, into, pl.ds(0, rows)],
            send_sem=hs.at[app, side],
            recv_sem=hr.at[app, into],
            device_id=target[side],
            device_id_type=MESH,
        )

    for side in range(sides):

        @pl.when(jnp.logical_not(has[side]))
        def _(side=side):
            for app in range(4):
                rbuf[app, side] = jnp.zeros((vecs + 8, edges), F32)

    lane_id = lax.broadcasted_iota(jnp.int32, (8, cells), 1)
    mask[...] = jnp.where(lane_id < live_ref[0, 0], 1.0, 0.0)

    def store_parts(begin, x, into=vp):
        hi, lo = split(x)
        for t in range(x.shape[1] // block):
            lanes = slice(t * block, (t + 1) * block)
            into[begin // block + t, 0:vecs, :] = hi[:, lanes]
            into[begin // block + t, vecs:group_rows, :] = lo[:, lanes]

    def all_parts(src):
        return jnp.concatenate([src[t] for t in range(blocks)], axis=1)

    step = 128
    position = lax.broadcasted_iota(jnp.int32, (step, edges), 0).astype(F32).astype(BF16)
    one, none = jnp.ones((step, edges), BF16), jnp.zeros((step, edges), BF16)

    @pl.loop(0, cells // step)
    def _(t):
        base = pl.multiple_of(t * step, step)
        for side in range(sides):
            inside = edges_ref[0, 0, side : side + 1, :] - base
            inside = jnp.where((inside >= 0) & (inside < step), inside, 255)
            key = jnp.broadcast_to(inside.astype(F32), (step, edges)).astype(BF16)
            pick[pl.ds(base, step), side * edges : (side + 1) * edges] = jnp.where(
                position == key, one, none
            )

    load.wait()
    start = rest[...] * mask[0:1, :]
    fa[...] = start
    store_parts(0, start)

    chunk = 512
    chunks = [slice(q * chunk, (q + 1) * chunk) for q in range(cells // chunk)]
    pair = 2 * edges

    def gather(k, src):
        got = dot(all_parts(src), pick[:, k * pair : (k + 1) * pair])
        return got[0:vecs] + got[vecs:]

    def send(app, k, values):
        for i in range(2):
            sbuf[app, 2 * k + i, 0:vecs, :] = values[:, i * edges : (i + 1) * edges]
        for i in range(2):

            @pl.when(has[2 * k + i])
            def _(i=i):
                halo(app, 2 * k + i, facing[2 * k + i]).start()

    def sent(app, k):
        return jnp.concatenate([sbuf[app, 2 * k, 0:vecs, :], sbuf[app, 2 * k + 1, 0:vecs, :]], axis=1)

    def multiply(use, width):
        for n in range(blocks):
            got = dot(
                jnp.concatenate([vp[cols_ref[0, s, 0, n]] for s in range(stored)], axis=1),
                wts[n],
                NT,
            )
            use(
                slice(n * block, (n + 1) * block),
                got[0:vecs, 0:width] + got[vecs:, 0:width] + got[0:vecs, width:],
            )

    def receive(app, factor):
        for side in range(sides):

            @pl.when(has[side])
            def _(side=side):
                halo(app, side, side).wait_recv()

        for side in range(sides):
            came = rbuf[app, side, 0:vecs, :]
            if factor is not None:
                came = came * (rbuf[app, side, vecs : vecs + 1, 0:1] * factor)
            hi, lo = split(came)
            lanes = slice(side * edges, (side + 1) * edges)
            inp[0:vecs, lanes] = hi
            inp[vecs:group_rows, lanes] = lo

    def across(k):
        got = dot(inp[...], same[:, k * pair : (k + 1) * pair])
        return got[0:vecs] + got[vecs:]

    def landed(sl):
        got = dot(inp[...], place[:, sl])
        return got[0:vecs] + got[vecs:]

    def exchange(kind, buf, peer, me, size):
        def one(d):
            return pltpu.make_async_remote_copy(
                src_ref=buf.at[me],
                dst_ref=buf.at[me],
                send_sem=cs.at[kind, d],
                recv_sem=cr.at[kind, d],
                device_id=peer(d),
                device_id_type=MESH,
            )

        return [one(d) for d in far_first(size)]

    def wait_from(kind, buf, me, size, peer, d):
        src = lax.rem(me + size - d, size)
        return pltpu.make_async_remote_copy(
            src_ref=buf.at[src],
            dst_ref=buf.at[src],
            send_sem=cs.at[kind, d],
            recv_sem=cr.at[kind, d],
            device_id=peer(d),
            device_id_type=MESH,
        )

    ahead = gather(1, vp)
    pl.semaphore_wait(barrier, size_x + size_y - 2)
    send(0, 1, ahead)
    send(0, 0, gather(0, vp))

    lane = lax.broadcasted_iota(jnp.int32, (128, 128), 1).astype(F32).astype(BF16)
    zero = jnp.zeros((128, 128), BF16)

    def apart(ends):
        high = lax.shift_right_logical(ends, 7)
        return high.astype(F32), (ends - high * 128).astype(F32)

    def down(at):
        side, from_edge = at // edges, at % edges
        ends = edges_ref[0, 0, side : side + 1, from_edge : from_edge + 128]
        wide = [
            jnp.broadcast_to(
                jnp.transpose(jnp.broadcast_to(x, (8, 128)))[:, 0:1], (128, 128)
            ).astype(BF16)
            for x in apart(ends)
        ]
        return wide[0], wide[1], jnp.where(wide[1] == lane, jnp.ones((128, 128), BF16), zero)

    counts = [jnp.zeros((16, 128), F32) for _ in range(cells // 128)]
    for at in range(0, ends_all, 128):
        high, _, spot = down(at)
        flag = jnp.where(has[at // edges], 1.0, 0.0).astype(F32)
        for t in range(cells // 128):
            hit = jnp.where(high == jnp.full((128, 128), t, BF16), spot, zero)
            place[at : at + 128, t * 128 : (t + 1) * 128] = hit
            some = hit[0:16]
            for r in range(16, 128, 16):
                some = some + hit[r : r + 16]
            counts[t] = counts[t] + flag * some.astype(F32)
    for t in range(cells // 128):
        deg[:, t * 128 : (t + 1) * 128] = jnp.broadcast_to(
            jnp.sum(counts[t], axis=0, keepdims=True), (8, 128)
        )

    for t in range(blocks):
        vm[t] = mask[:, t * block : (t + 1) * block]
    ones = jnp.ones((16, block), BF16)
    for n in range(blocks):
        fetches[n].wait()
        heavy = jnp.zeros((block, block), F32)
        for s in range(stored):
            w = raw[n, s]
            hi, lo = split(w)
            wts[n, 0:block, s * block : (s + 1) * block] = hi
            wts[n, block : 2 * block, s * block : (s + 1) * block] = lo
            heavy = heavy + w * vm[cols_ref[0, s, 0, n]][0:1, :]
        here = slice(n * block, (n + 1) * block)
        got = dot(ones, jnp.concatenate(split(heavy), axis=0), NT)
        own = got[0:8, 0:block] + got[0:8, block:]
        deg[:, here] = mask[:, here] * (deg[:, here] + own)
    top = jnp.max(deg[...], axis=1, keepdims=True)
    mxa[me_y] = jnp.broadcast_to(top, (8, 128))
    for c in exchange(0, mxa, peer_y, me_y, size_y):
        c.start()
    local = 2.0 * top[0:1, :]
    local = jnp.where(local > 0.0, local, 1.0)
    shrink = 1.0 / local
    for side in range(sides):
        sbuf[scaled, side, vecs : vecs + 8, :] = jnp.broadcast_to(local, (8, edges))

    def keep(here, x, for_edges=True):
        rest[:, here] = x
        if for_edges:
            store_parts(here.start, x, rp)

    def local_z(here, wv):
        keep(here, mask[0:1, here] * (deg[0:1, here] * fa[:, here] - wv) * shrink)

    multiply(local_z, block)

    for at in range(0, ends_all, 128):
        high, low, _ = down(at)
        for t in range(0, ends_all, 128):
            other = edges_ref[0, 0, t // edges : t // edges + 1, t % edges : t % edges + 128]
            far_high, far_low = (
                jnp.broadcast_to(x, (128, 128)).astype(BF16) for x in apart(other)
            )
            meet = jnp.where(low == far_low, jnp.ones((128, 128), BF16), zero)
            same[at : at + 128, t : t + 128] = jnp.where(high == far_high, meet, zero)

    ahead = [gather(0, rp), gather(1, rp)]
    receive(0, None)
    for k in (1, 0):
        send(1, k, ahead[k] - across(k) * shrink)
    for d in range(1, size_y):
        wait_from(0, mxa, me_y, size_y, peer_y, d).wait_recv()
    mxb[me_x] = jnp.max(mxa[...], axis=0)
    for c in exchange(1, mxb, peer_x, me_x, size_x):
        c.start()
    for sl in chunks:
        z = rest[:, sl] - mask[0:1, sl] * landed(sl) * shrink
        fb[:, sl] = z
        store_parts(sl.start, z)

    def local_lz(here, wv):
        keep(here, mask[0:1, here] * (deg[0:1, here] * fb[:, here] - wv))

    multiply(local_lz, block)
    ahead = [gather(0, rp), gather(1, rp)]
    receive(1, shrink)
    for d in range(1, size_x):
        wait_from(1, mxb, me_x, size_x, peer_x, d).wait_recv()
    upper = 2.0 * jnp.max(mxb[...], axis=0)[0:1, 0:1]
    lower = LOWER_FRACTION * upper
    half_width = (upper - lower) / 2.0
    centre = (upper + lower) / 2.0
    over = 1.0 / half_width
    ratio = centre * over
    grow = local * over

    def y2_of(lz, z, y0):
        return 2.0 * (grow * (lz * over) - (2.0 * ratio * grow) * z + (ratio * ratio) * y0) - y0

    for k in (1, 0):
        send(2, k, y2_of(ahead[k] - across(k), sent(1, k), sent(0, k)))
    for sl in chunks:
        lz = rest[:, sl] - mask[0:1, sl] * landed(sl)
        z, y0 = fb[:, sl], fa[:, sl]
        y2 = y2_of(lz, z, y0)
        fb[:, sl] = y2
        fa[:, sl] = grow * z - ratio * y0
        store_parts(sl.start, y2)

    twice = 2.0 * over
    previous, current = fa, fb
    for app in (2, 3):

        def local_next(here, wv, app=app, previous=previous, current=current):
            y = current[:, here]
            lap = mask[0:1, here] * (deg[0:1, here] * y - wv)
            keep(here, twice * (lap - centre * y) - previous[:, here], app == 2)

        multiply(local_next, block)
        if app == 2:
            ahead = [gather(0, rp), gather(1, rp)]
        receive(app, None)
        if app == 2:
            for k in (1, 0):
                send(3, k, ahead[k] - twice * across(k))
        for sl in chunks:
            new = rest[:, sl] - mask[0:1, sl] * (twice * landed(sl))
            if app == 2:
                previous[:, sl] = new
            store_parts(sl.start, new)
        previous, current = current, previous

    filtered = pltpu.make_async_copy(vp, parts_ref, psem)
    filtered.start()
    both = all_parts(vp)
    full = dot(both, both, NT)
    gram = full[0:vecs, 0:vecs] + full[0:vecs, vecs:] + full[vecs:, 0:vecs] + full[vecs:, vecs:]
    gram = jnp.concatenate([gram, jnp.zeros((vecs, 128 - vecs), F32)], axis=1)
    owners = vecs // 8
    for p in range(owners):
        gpart[p] = gram[8 * p : 8 * p + 8, :]

    def to_owner(p):
        return pltpu.make_async_remote_copy(
            src_ref=gpart.at[p],
            dst_ref=gr1.at[me_y],
            send_sem=cs.at[2, p],
            recv_sem=cr.at[2, me_y],
            device_id={"gx": me_x, "gy": p},
            device_id_type=MESH,
        )

    def from_member(q):
        return pltpu.make_async_remote_copy(
            src_ref=gr1.at[q],
            dst_ref=gr1.at[q],
            send_sem=cs.at[2, q],
            recv_sem=cr.at[2, q],
            device_id={"gx": me_x, "gy": q},
            device_id_type=MESH,
        )

    def from_owner(p):
        return pltpu.make_async_remote_copy(
            src_ref=gfull.at[p],
            dst_ref=gfull.at[p],
            send_sem=cs.at[4, 0],
            recv_sem=cr.at[4, lax.rem(me_y + size_y - p, size_y)],
            device_id={"gx": me_x, "gy": p},
            device_id_type=MESH,
        )

    for p in range(owners):

        @pl.when(me_y != p)
        def _(p=p):
            to_owner(p).start()

    @pl.when(me_y < owners)
    def _():
        gr1[me_y] = gpart[me_y]
        for q in range(size_y):

            @pl.when(me_y != q)
            def _(q=q):
                from_member(q).wait_recv()

        gr2[me_x] = jnp.sum(gr1[...], axis=0)
        for c in exchange(3, gr2, peer_x, me_x, size_x):
            c.start()
        for d in range(1, size_x):
            wait_from(3, gr2, me_x, size_x, peer_x, d).wait_recv()
        gfull[me_y] = jnp.sum(gr2[...], axis=0)
        for c in exchange(4, gfull, peer_y, me_y, size_y):
            c.start()

    for app in range(4):
        for side in range(sides):

            @pl.when(has[side])
            def _(app=app, side=side):
                halo(app, side, facing[side]).wait_send()

    for c in exchange(0, mxa, peer_y, me_y, size_y) + exchange(1, mxb, peer_x, me_x, size_x):
        c.wait_send()
    for p in range(owners):

        @pl.when(me_y != p)
        def _(p=p):
            to_owner(p).wait_send()

    for p in range(owners):

        @pl.when(me_y != p)
        def _(p=p):
            from_owner(p).wait_recv()

    @pl.when(me_y < owners)
    def _():
        for c in exchange(3, gr2, peer_x, me_x, size_x) + exchange(4, gfull, peer_y, me_y, size_y):
            c.wait_send()

    filtered.wait()


def finish_kernel(scale, gram_ref, parts_ref, out_ref, work, elem, inv, parts, result, psem, osem):
    vecs, cells = out_ref.shape[2:]
    fetch = pltpu.make_async_copy(parts_ref, parts, psem)
    fetch.start()
    work[...] = gram_ref[...]
    inverse_factor(work, elem, inv, scale, vecs)
    hi, lo = split(inv[...])
    hi, lo = hi[:, 0:vecs], lo[:, 0:vecs]
    left = jnp.concatenate(
        [jnp.concatenate([hi, hi], axis=1), jnp.concatenate([lo, lo], axis=1)], axis=0
    )
    fetch.wait()
    blocks, chunks = parts.shape[0], osem.shape[0]
    each, width = blocks // chunks, cells // chunks
    writes = []
    for q in range(chunks):
        got = dot(left, jnp.concatenate([parts[q * each + t] for t in range(each)], axis=1))
        result[q] = got[0:vecs] + got[vecs:]
        writes.append(
            pltpu.make_async_copy(
                result.at[q], out_ref.at[0, 0, :, pl.ds(q * width, width)], osem.at[q]
            )
        )
        writes[q].start()
    for w in writes:
        w.wait()


def per_device(size_x, size_y, basis, block_vals, block_cols, edge_rows, live_counts):
    blocks, stored, block = block_vals.shape[2:5]
    vecs, cells = basis.shape[2:]
    sides, edges = edge_rows.shape[2:]
    ends = sides * edges
    vmem = pltpu.VMEM
    field = vmem((vecs, cells), F32)
    scratch = [
        vmem((blocks, 2 * vecs, block), BF16),
        vmem((blocks, 2 * vecs, block), BF16),
        vmem((blocks, stored, block, block), F32),
        vmem((blocks, 2 * block, stored * block), BF16),
        vmem((cells, ends), BF16),
        vmem((ends, cells), BF16),
        vmem((ends, ends), BF16),
        vmem((blocks, 8, block), F32),
        vmem((2 * vecs, ends), BF16),
        field,
        field,
        field,
        vmem((8, cells), F32),
        vmem((8, cells), F32),
        vmem((4, sides, vecs + 8, edges), F32),
        vmem((4, sides, vecs + 8, edges), F32),
        vmem((size_y, 8, 128), F32),
        vmem((size_x, 8, 128), F32),
        vmem((vecs // 8, 8, 128), F32),
        vmem((size_y, 8, 128), F32),
        vmem((size_x, 8, 128), F32),
        pltpu.SemaphoreType.DMA((blocks,)),
        pltpu.SemaphoreType.DMA,
        pltpu.SemaphoreType.DMA,
        pltpu.SemaphoreType.DMA((4, sides)),
        pltpu.SemaphoreType.DMA((4, sides)),
        pltpu.SemaphoreType.DMA((5, max(size_x, size_y))),
        pltpu.SemaphoreType.DMA((5, max(size_x, size_y))),
    ]
    in_vmem = pl.BlockSpec(memory_space=vmem)
    in_hbm = pl.BlockSpec(memory_space=pl.ANY)
    in_smem = pl.BlockSpec(memory_space=pltpu.SMEM)
    parts, gram = pl.pallas_call(
        lambda *refs: filter_kernel(size_x, size_y, *refs),
        out_shape=[
            jax.ShapeDtypeStruct((blocks, 2 * vecs, block), BF16),
            jax.ShapeDtypeStruct((vecs // 8, 8, 128), F32),
        ],
        in_specs=[in_smem, in_smem, in_hbm, in_vmem, in_hbm],
        out_specs=[in_hbm, in_vmem],
        scratch_shapes=scratch,
        compiler_params=pltpu.CompilerParams(
            collective_id=0, has_side_effects=True, vmem_limit_bytes=60 * 2**20
        ),
        name="filter_and_gram",
    )(live_counts, jnp.transpose(block_cols, (0, 3, 1, 2)), basis, edge_rows, block_vals)
    steps = 4
    return pl.pallas_call(
        lambda *refs: finish_kernel(math.sqrt(cells * size_x * size_y), *refs),
        out_shape=jax.ShapeDtypeStruct(basis.shape, F32),
        in_specs=[in_vmem, pl.BlockSpec(memory_space=pl.ANY)],
        out_specs=pl.BlockSpec(memory_space=pl.ANY),
        scratch_shapes=[
            vmem(gram.shape, F32),
            vmem((8, 8, 128), F32),
            vmem((vecs, 128), F32),
            vmem(parts.shape, BF16),
            vmem((steps, vecs, cells // steps), F32),
            pltpu.SemaphoreType.DMA,
            pltpu.SemaphoreType.DMA((steps,)),
        ],
        compiler_params=pltpu.CompilerParams(vmem_limit_bytes=60 * 2**20),
        name="factor_and_encode",
    )(gram, parts)


def solution(mesh):
    size_x, size_y = mesh.shape["gx"], mesh.shape["gy"]
    in_specs = (
        P("gx", "gy", None, None),
        P("gx", "gy", None, None, None, None),
        P("gx", "gy", None, None),
        P("gx", "gy", None, None),
        P("gx", "gy"),
    )
    out_specs = P("gx", "gy", None, None)
    return jax.shard_map(
        lambda *args: per_device(size_x, size_y, *args),
        mesh=mesh,
        in_specs=in_specs,
        out_specs=out_specs,
        check_vma=False,
    )
```
